128 devices in a mesh: row: 8 (over x, core), col: 16 (over z, y).
Axes of the slice: x: 4, y: 4, z: 4, core: 2. Of those that a mesh axis runs over, the one named last changes fastest.
Arguments:
- features: bfloat16 [524288, 512], P(('row', 'col')), may hold values from -6 to 6
- w_first: bfloat16 [1024, 512], replicated, may hold values from -0.1875 to 0.1875
- w_second: bfloat16 [1024, 512], replicated, may hold values from -0.1875 to 0.1875
- send_rows: int32 [128, 8, 256], P(('row', 'col')), may hold values from 0 to 4095
- halo_count: int32 [128, 8], P(('row', 'col')), may hold values from 0 to 256, as said below
- hub_owner: int32 [8, 2048, 1], P('row'), may hold values from 0 to 15; in each aligned block of 2048 rows (0 to 2047, 2048 to 4095, ..., all dimensions but the last counted through in order) at most 384 rows name the same one
- hub_row: int32 [8, 2048], P('row'), may hold values from 0 to 4095
- local_cols: int32 [128, 32, 2], P(('row', 'col')), may hold values from 0 to 31
- local_tiles: bfloat16 [128, 32, 2, 128, 128], P(('row', 'col')), may hold values from 0 to 1, as said below
- remote_cols: int32 [128, 32, 2], P(('row', 'col')), may hold values from 0 to 31, as said below
- remote_tiles: bfloat16 [128, 32, 2, 128, 128], P(('row', 'col')), may hold values from 0 to 1
Outputs:
- embeddings: bfloat16 [524288, 512], P(('row', 'col'))
The draws below stay inside these ranges and needn't reach their ends.
Inputs may be any that keep to these rules, and one draw needn't show every extreme that they name: `halo_count`: zero where p is d's own row index; some entry equals 256. `hub_owner`: in each row of partitions no owner holds more than 384 hubs, and some owner holds exactly 384. `remote_cols`: each partition's tiles name every block of its remote store at least once. The diagonal of local_tiles[d, b, 0] lies in 0.5 to 1.
All inputs are finite; a program needn't handle non-finite values.
Results may differ from the reference program's by a relative error of at most 0.005.
Values may be sent and summed in bfloat16 or wider, within the bound.
No kernel may reach another device: no remote copies, remote signals or barrier semaphores. Data moves between devices by JAX's collectives and lax.ppermute only.
A program may use at most 128 MiB of HBM per device.

```python
import math
import jax
import jax.numpy as jnp
import numpy as np
from jax import lax

F = 512
NODES_DEV = 4096
HALO_CAP = 256
HUBS = 2048
TB = 128
TL = 2
TR = 2
NODES = 524288
BLOCKS = 32
REMOTE_BLOCKS = 32
HUB_CAP = 384
N_ROW = 8
N_COL = 16
DEVICES = 128


def draw_halo_count(key, part):
    key = jax.random.fold_in(key, 11)
    counts = jax.random.randint(key, (DEVICES, N_ROW), HALO_CAP // 4, HALO_CAP + 1, dtype=jnp.int32)
    own_row = jnp.arange(DEVICES, dtype=jnp.int32)[:, None] // N_COL
    peer_rows = jnp.arange(N_ROW, dtype=jnp.int32)[None, :]
    counts = jnp.where(peer_rows == own_row, 0, counts)
    return counts.at[0, 1].set(HALO_CAP)


def draw_local_tiles(key, part):
    key = jax.random.fold_in(key, 21)
    key_mask, key_vals, key_diag = jax.random.split(key, 3)
    tile_shape = (DEVICES, BLOCKS, TL, TB, TB)
    keep_draw = jax.random.uniform(key_mask, tile_shape) < 0.125
    values = jax.random.uniform(key_vals, tile_shape, minval=0.05, maxval=1.0)
    tiles = jnp.where(keep_draw, values, 0.0)
    diagonal = jax.random.uniform(key_diag, (DEVICES, BLOCKS, TB), minval=0.5, maxval=1.0)
    on_diagonal = jnp.eye(TB, dtype=bool)
    first_tiles = jnp.where(on_diagonal, diagonal[..., None], tiles[:, :, 0])
    tiles = tiles.at[:, :, 0].set(first_tiles)
    return tiles.astype(jnp.bfloat16)


def draw_remote_tiles(key, part):
    key = jax.random.fold_in(key, 27)
    key_mask, key_vals = jax.random.split(key, 2)
    tile_shape = (DEVICES, BLOCKS, TR, TB, TB)
    keep_draw = jax.random.uniform(key_mask, tile_shape) < 0.125
    values = jax.random.uniform(key_vals, tile_shape, minval=0.05, maxval=1.0)
    return jnp.where(keep_draw, values, 0.0).astype(jnp.bfloat16)


def draw_remote_cols(key, part):
    key = jax.random.fold_in(key, 31)
    device_keys = jax.random.split(key, DEVICES)
    shuffled = jax.vmap(lambda one_key: jax.random.permutation(one_key, BLOCKS * TR))(device_keys)
    return (shuffled % REMOTE_BLOCKS).astype(jnp.int32).reshape(DEVICES, BLOCKS, TR)


def touch_ends(drawn, stream_key, least, top_value):
    extent = drawn.shape
    spot = [jax.random.randint(jax.random.fold_in(stream_key, axis), (), 0, extent[axis]) for axis in range(len(extent))]
    drawn = drawn.at[tuple(spot)].set(least)
    longest = extent.index(max(extent))
    spot[longest] = (spot[longest] + 1) % extent[longest]
    return drawn.at[tuple(spot)].set(top_value)


def block_scale(own_key, dims, shards, low, top_value):
    loudness, own = 1.0, jax.random.fold_in(own_key, 6)
    for dim, shards_of in shards:
        draws = jnp.exp(jax.random.uniform(jax.random.fold_in(own, dim), (shards_of,), jnp.float32, low / len(shards), top_value / len(shards)))
        loudness = loudness * jnp.repeat(draws, dims[dim] // shards_of).reshape([-1 if axis == dim else 1 for axis in range(len(dims))])
    return loudness


def routed_block(rng, own, number, rows, number_of, top, limit, lean):
    sequence = jax.random.permutation(rng, number_of)
    crowded, common = shares(number_of, rows * top, limit, lean, True), shares(number_of, rows * top, limit, lean, False)
    places = jnp.arange(number_of)

    def named(sizes, turn):
        used = int((sizes > 0).sum())
        fixed = max(1, used // 4)
        passed = fixed + (places - fixed + turn * (used - fixed)) % max(1, number_of - fixed)
        return jnp.zeros((number_of,), jnp.int32).at[sequence[jnp.where(places < fixed, places, passed)]].set(jnp.asarray(sizes, jnp.int32))

    sizes = jnp.where(number % 4 == 0, named(crowded, number // 4), named(common, number - number // 4 - 1))
    mixed = jax.random.permutation(jax.random.fold_in(own, 3), number_of)
    donor, taker = mixed[0:number_of // 2 * 2:2], mixed[1:number_of // 2 * 2:2]
    margin = jnp.minimum(sizes[donor] - 1, limit - sizes[taker]) // 2
    margin = jnp.where((donor == sequence[0]) | (taker == sequence[0]) | (sizes[taker] == 0), 0, jnp.maximum(margin, 0))
    passed = jax.random.randint(jax.random.fold_in(own, 4), (number_of // 2,), 0, 1 << 20) % (margin + 1)
    sizes = sizes.at[donor].add(-passed).at[taker].add(passed)
    items = jnp.searchsorted(jnp.cumsum(sizes), jnp.arange(rows * top), side="right").astype(jnp.int32)
    listing = items.reshape(top, rows).T
    listing = listing[jax.random.permutation(jax.random.fold_in(own, 1), rows)]
    turn = jax.random.randint(jax.random.fold_in(own, 2), (rows, 1), 0, top)
    return jnp.take_along_axis(listing, (jnp.arange(top)[None, :] + turn) % top, axis=1)


def shares(number_of, total, bound, skew, full):
    weights = [(1 << 20) // math.isqrt(grade ** skew) + 1 for grade in range(1, number_of + 1)]
    largest = bound if full else min(bound, max(-(-total // number_of), total * weights[0] // sum(weights)))
    least = 1 if total - largest >= number_of - 1 else 0
    holding, surplus = [largest] + [least] * (number_of - 1), total - largest - least * (number_of - 1)
    while surplus > 0:
        candidates = [i for i in range(1, number_of) if holding[i] < largest] or [i for i in range(1, number_of) if holding[i] < bound]
        mass, budget = sum([weights[i] for i in candidates]), surplus
        for i in candidates:
            more = min(bound - holding[i], max(1, budget * weights[i] // mass), surplus)
            holding[i] = holding[i] + more
            surplus = surplus - more
    return np.array(holding)


def noise(rng, dims, width, bound, pieces=(), kind=jnp.bfloat16):
    factor_of = block_scale(rng, dims, pieces, -0.22, 0.18) if pieces else 1.0
    entries = jax.random.normal(rng, dims, jnp.float32) * width * factor_of
    return jnp.minimum(jnp.maximum(entries, -bound), bound).astype(kind)


def setup_inputs(seed: int = 0) -> dict:
    key_list = jax.random.split(jax.random.key(seed), 12)
    features = noise(key_list[0], (NODES, F), 1.0, 6.0, ((0, 128),))
    w_first = noise(key_list[1], (2 * F, F), (2 * F) ** -0.5, 0.1875)
    w_second = noise(key_list[2], (2 * F, F), (2 * F) ** -0.5, 0.1875)
    send_rows = touch_ends(jax.random.randint(key_list[3], (DEVICES, N_ROW, HALO_CAP), 0, NODES_DEV), jax.random.fold_in(key_list[3], 1), 0, NODES_DEV - 1).astype(jnp.int32)
    halo_count = draw_halo_count(jax.random.fold_in(key_list[11], 71), 0)
    hub_owner_keys = jax.random.split(jax.random.fold_in(key_list[5], 1), N_ROW * HUBS // HUBS)
    hub_owner_turns = jax.random.permutation(jax.random.fold_in(key_list[5], 3), N_ROW * HUBS // HUBS)
    hub_owner = jax.vmap(lambda own, number: routed_block(jax.random.fold_in(key_list[5], 2), own, number, HUBS, N_COL, 1, HUB_CAP, 2))(hub_owner_keys, hub_owner_turns).reshape((N_ROW, HUBS, 1))
    hub_row = touch_ends(jax.random.randint(key_list[6], (N_ROW, HUBS), 0, NODES_DEV), jax.random.fold_in(key_list[6], 1), 0, NODES_DEV - 1).astype(jnp.int32)
    local_cols = touch_ends(jax.random.randint(key_list[7], (DEVICES, BLOCKS, TL), 0, BLOCKS), jax.random.fold_in(key_list[7], 1), 0, BLOCKS - 1).astype(jnp.int32)
    local_tiles = draw_local_tiles(jax.random.fold_in(key_list[11], 71), 0)
    remote_cols = draw_remote_cols(jax.random.fold_in(key_list[11], 71), 0)
    remote_tiles = draw_remote_tiles(jax.random.fold_in(key_list[11], 71), 0)
    return {"features": features, "w_first": w_first, "w_second": w_second, "send_rows": send_rows, "halo_count": halo_count, "hub_owner": hub_owner, "hub_row": hub_row, "local_cols": local_cols, "local_tiles": local_tiles, "remote_cols": remote_cols, "remote_tiles": remote_tiles}


def sage_layer(node_table, weight, send_rows, halo_count, hub_owner, hub_row, local_cols, local_tiles, remote_cols, remote_tiles):
    send_table = send_rows.reshape(N_ROW, N_COL, N_ROW, HALO_CAP)
    count_table = halo_count.reshape(N_ROW, N_COL, N_ROW)
    slot_ids = jnp.arange(HALO_CAP, dtype=jnp.int32)
    peer_ids = jnp.arange(N_ROW, dtype=jnp.int32)
    weight_f = weight.astype(jnp.float32)

    def one_device(device):
        row_index = device // N_COL
        col_index = device % N_COL
        own_rows = node_table[row_index, col_index]
        column_rows = node_table[:, col_index]
        sent_rows = send_table[:, col_index, row_index]
        halo_rows = column_rows[peer_ids[:, None], sent_rows]
        valid_mask = slot_ids[None, :] < count_table[:, col_index, row_index][:, None]
        halo_rows = jnp.where(valid_mask[:, :, None], halo_rows, jnp.zeros((), jnp.bfloat16))
        group_rows = node_table[row_index]
        hub_feats = group_rows[hub_owner[row_index, :, 0], hub_row[row_index]]
        remote = jnp.concatenate([halo_rows.reshape(-1, F), hub_feats], axis=0)
        remote_blocks = remote.reshape(REMOTE_BLOCKS, TB, F).astype(jnp.float32)
        mark_vals = jnp.concatenate([valid_mask.reshape(-1).astype(jnp.float32), jnp.ones((HUBS,), jnp.float32)])
        mark_blocks = mark_vals.reshape(REMOTE_BLOCKS, TB)
        own_blocks = own_rows.reshape(BLOCKS, TB, F).astype(jnp.float32)
        local_vals = local_tiles[device].astype(jnp.float32)
        remote_vals = remote_tiles[device].astype(jnp.float32)
        local_index = local_cols[device]
        remote_index = remote_cols[device]
        summed = jnp.einsum('btij,btjf->bif', local_vals, own_blocks[local_index])
        summed = summed + jnp.einsum('btij,btjf->bif', remote_vals, remote_blocks[remote_index])
        denominator = lax.optimization_barrier(jnp.sum(local_vals, axis=(1, 3))) + jnp.einsum('btij,btj->bi', remote_vals, mark_blocks[remote_index])
        averaged = (summed / denominator[:, :, None]).astype(jnp.bfloat16).reshape(NODES_DEV, F)
        preact = jnp.dot(own_rows.astype(jnp.float32), weight_f[:F]) + jnp.dot(averaged.astype(jnp.float32), weight_f[F:])
        activated = jnp.maximum(preact, 0.0)
        scaled = activated * lax.rsqrt(lax.optimization_barrier(jnp.mean(activated * activated, axis=-1, keepdims=True)) + 1e-05)
        return scaled.astype(jnp.bfloat16)
    result = lax.map(one_device, jnp.arange(DEVICES, dtype=jnp.int32))
    return result.reshape(N_ROW, N_COL, NODES_DEV, F)

def reference(features, w_first, w_second, send_rows, halo_count, hub_owner, hub_row, local_cols, local_tiles, remote_cols, remote_tiles):
    node_table = features.reshape(N_ROW, N_COL, NODES_DEV, F)
    for weight in (w_first, w_second):
        node_table = sage_layer(node_table, weight, send_rows, halo_count, hub_owner, hub_row, local_cols, local_tiles, remote_cols, remote_tiles)
    return node_table.reshape(NODES, F)
```

```python
import functools

import jax
import jax.numpy as jnp
from jax import lax
from jax.experimental import pallas as pl
from jax.experimental.pallas import tpu as pltpu
from jax.sharding import PartitionSpec as P

F32 = jnp.float32
BF16 = jnp.bfloat16
I32 = jnp.int32
VMEM_LIMIT = 58 * 1024 * 1024
TB = 128
ROWS = 8
COLS = 16
SIDE = 4
HALO = 256
NOTE = 16
HUBS = 2048
HUB_CAP = 384
TALL = 512


def params():
    return pltpu.CompilerParams(vmem_limit_bytes=VMEM_LIMIT)


def cost():
    return pl.CostEstimate(flops=1000, bytes_accessed=1000, transcendentals=0)


def vmem():
    return pl.BlockSpec(memory_space=pltpu.VMEM)


def smem():
    return pl.BlockSpec(memory_space=pltpu.SMEM)


def hbm():
    return pl.BlockSpec(memory_space=pl.ANY)


def whole(*shape):
    return pl.BlockSpec(shape, lambda i: (0,) * len(shape))


def band(tall, *rest):
    return pl.BlockSpec((tall, *rest), lambda i: (i,) + (0,) * len(rest))


def shape(dtype, *dims):
    return jax.ShapeDtypeStruct(dims, dtype)


def iota(dims, dim):
    return lax.broadcasted_iota(I32, dims, dim)


def widen(rows, wide, first):
    lanes = rows.shape[1] // TB
    for j in range(lanes):
        wide[pl.ds(first * lanes + j, rows.shape[0], stride=lanes), :] = rows[:, j * TB : (j + 1) * TB]


def move_row(source, row, target, slot):
    lanes = 4
    target[pl.ds(pl.multiple_of(slot * lanes, lanes), lanes), :] = source[
        pl.ds(pl.multiple_of(row * lanes, lanes), lanes), :
    ]


def write_index(my_col, owner, rows, send_ref, pos_ref):
    chunks = HUBS // TB
    owner_id = iota((COLS, TB), 0)
    masks = [jnp.where(owner[:, c * TB : (c + 1) * TB] == owner_id, 1.0, 0.0) for c in range(chunks)]
    earlier = jnp.where(iota((TB, TB), 0) < iota((TB, TB), 1), 1.0, 0.0).astype(BF16)
    inside = jnp.dot(jnp.concatenate(masks, axis=0).astype(BF16), earlier, preferred_element_type=F32)
    running = jnp.zeros((COLS, 1), F32)
    ranks = []
    for c in range(chunks):
        rank = inside[c * COLS : (c + 1) * COLS, :] + running
        ranks.append(jnp.sum(masks[c] * rank, axis=0, keepdims=True))
        running = running + jnp.sum(masks[c], axis=1, keepdims=True)
    rank = jnp.concatenate(ranks, axis=0).astype(I32)
    who = jnp.concatenate([owner[:, c * TB : (c + 1) * TB] for c in range(chunks)], axis=0)
    local = jnp.concatenate([rows[:, c * TB : (c + 1) * TB] for c in range(chunks)], axis=0).astype(F32)
    slot = jnp.where(who == my_col, rank, -1)
    for k in range(HUB_CAP // TB):
        wanted = iota((TB, TB), 0) + k * TB
        total = jnp.zeros((TB, TB), F32)
        for c in range(chunks):
            total = total + jnp.where(slot[c : c + 1, :] == wanted, local[c : c + 1, :], 0.0)
        send_ref[k * TB : (k + 1) * TB, :] = jnp.sum(total, axis=1, keepdims=True).astype(I32)
    pos_ref[0:chunks, :] = who * HUB_CAP + rank
    held = jnp.concatenate([jnp.broadcast_to(running, (COLS, TB)), jnp.zeros((TB - COLS, TB), F32)], axis=0)
    pos_ref[chunks : chunks + 8, :] = held.T[0:8, :].astype(I32)


def add_picked(step, send_ref, rows, total):
    wanted = send_ref[...] - step * TALL
    chosen = jnp.where(wanted == iota((HUB_CAP, TALL), 1), 1.0, 0.0).astype(BF16)
    part = jnp.dot(chosen, rows, preferred_element_type=F32)

    @pl.when(step == 0)
    def _():
        total[...] = part

    @pl.when(step > 0)
    def _():
        total[...] = total[...] + part


def hub_kernel(place_ref, owner_ref, row_ref, table_ref, out_ref, send_ref, pos_ref, total):
    step = pl.program_id(0)

    @pl.when(step == 0)
    def _():
        write_index(place_ref[1], owner_ref[...], row_ref[...], send_ref, pos_ref)

    add_picked(step, send_ref, table_ref[...], total)

    @pl.when(step == pl.num_programs(0) - 1)
    def _():
        out_ref[...] = total[...].astype(BF16)


def hub_start(place, owner, rows, table):
    nodes, width = table.shape
    listed = HUBS // TB + 8
    return pl.pallas_call(
        hub_kernel,
        grid=(nodes // TALL,),
        in_specs=[smem(), whole(1, HUBS), whole(1, HUBS), band(TALL, width)],
        out_specs=[whole(HUB_CAP, width), whole(HUB_CAP, 1), whole(listed, TB)],
        out_shape=[shape(BF16, HUB_CAP, width), shape(I32, HUB_CAP, 1), shape(I32, listed, TB)],
        scratch_shapes=[pltpu.VMEM((HUB_CAP, width), F32)],
        compiler_params=params(),
        cost_estimate=cost(),
        name="hub_start",
    )(place, owner, rows, table)


def write_halos(noted, rows_ref, count_ref, wide, picked, out):
    lanes = 4
    unroll = 16
    height = HALO + (NOTE if noted else 0)
    for peer in range(ROWS):
        count = count_ref[peer]

        @pl.loop(0, (count + unroll - 1) // unroll)
        def _(group):
            for u in range(unroll):
                slot = group * unroll + u
                move_row(wide, rows_ref[peer * HALO + slot], picked, slot)

        for half in range(HALO // TB):
            live = iota((TB, TB), 0) + half * TB < count
            top = peer * height + half * TB
            for j in range(lanes):
                part = picked[pl.ds(half * TB * lanes + j, TB, stride=lanes), :]
                out[top : top + TB, j * TB : (j + 1) * TB] = jnp.where(live, part, 0.0).astype(BF16)
        if noted:
            top = peer * height + HALO
            out[top : top + NOTE, :] = jnp.full((NOTE, lanes * TB), count, I32).astype(F32).astype(BF16)


def halo_kernel(noted, rows_ref, count_ref, table_ref, out_ref, wide, picked):
    step = pl.program_id(0)
    widen(table_ref[...].astype(F32), wide, step * TALL)

    @pl.when(step == pl.num_programs(0) - 1)
    def _():
        write_halos(noted, rows_ref, count_ref, wide, picked, out_ref)


def halo_start(noted, rows, count, table):
    nodes, width = table.shape
    height = ROWS * (HALO + (NOTE if noted else 0))
    return pl.pallas_call(
        functools.partial(halo_kernel, noted),
        grid=(nodes // TALL,),
        in_specs=[smem(), smem(), band(TALL, width)],
        out_specs=whole(height, width),
        out_shape=shape(BF16, height, width),
        scratch_shapes=[pltpu.VMEM((nodes * width // TB, TB), F32), pltpu.VMEM((HALO * width // TB, TB), F32)],
        compiler_params=params(),
        cost_estimate=cost(),
        name="halo_start",
    )(rows, count, table)


def near_kernel(
    weighed, place_ref, cols_ref, far_ref, table_ref, halo_ref, tiles_ref, far_tiles_ref, weight_ref, *rest
):
    if weighed:
        near_ref, inverse_ref, averaged = rest
    else:
        inverse_ref, near_ref, averaged = rest
    step = pl.program_id(0)
    group = tiles_ref.shape[0]
    width = table_ref.shape[1]
    my_row = place_ref[0]
    height = halo_ref.shape[0] // ROWS
    for b in range(group):
        at = (step * group + b) * 2
        rights = []
        for t in range(2):
            rights.append(table_ref[pl.ds(pl.multiple_of(cols_ref[at + t] * TB, TB), TB), :])
        blocks = [far_ref[at + t] for t in range(2)]
        for block in blocks:
            top = jnp.where(
                block < 2 * ROWS, lax.div(block, 2) * height + lax.rem(block, 2) * TB, my_row * height
            )
            rights.append(halo_ref[pl.ds(pl.multiple_of(top, 16), TB), :])
        left = jnp.concatenate([tiles_ref[b, 0], tiles_ref[b, 1], far_tiles_ref[b, 0], far_tiles_ref[b, 1]], axis=1)
        total = jnp.dot(left, jnp.concatenate(rights, axis=0), preferred_element_type=F32)
        if weighed:
            mass = tiles_ref[b, 0].astype(F32) + tiles_ref[b, 1].astype(F32)
            for t in range(2):
                top = pl.multiple_of(lax.rem(lax.div(blocks[t], 2), ROWS) * height + HALO, 16)
                noted = halo_ref[pl.ds(top, NOTE), 0:TB].astype(F32)[0:1, :]
                is_hub = jnp.where(blocks[t] < 2 * ROWS, 0.0, 1024.0)
                slots = (iota((1, TB), 1) + lax.rem(blocks[t], 2) * TB).astype(F32)
                mass = mass + jnp.where(slots < noted + is_hub, far_tiles_ref[b, t].astype(F32), 0.0)
            inverse = 1.0 / jnp.sum(mass, axis=1, keepdims=True)
            inverse_ref[b * TB : (b + 1) * TB, :] = inverse
        else:
            inverse = inverse_ref[b * TB : (b + 1) * TB, :]
        averaged[b * TB : (b + 1) * TB, :] = (total * inverse).astype(BF16)
    own = table_ref[pl.ds(pl.multiple_of(step * TALL, TALL), TALL), :]
    near_ref[...] = jnp.dot(own, weight_ref[0:width, :], preferred_element_type=F32) + jnp.dot(
        averaged[...], weight_ref[width : 2 * width, :], preferred_element_type=F32
    )


def near_part(weighed, place, cols, far_cols, table, halos, tiles, far_tiles, weight, inverse=None):
    nodes, width = table.shape
    group = TALL // TB
    in_specs = [
        smem(),
        smem(),
        smem(),
        whole(nodes, width),
        whole(*halos.shape),
        band(group, 2, TB, TB),
        band(group, 2, TB, TB),
        whole(*weight.shape),
    ]
    args = [place, cols, far_cols, table, halos, tiles, far_tiles, weight]
    out_specs = [band(TALL, width)]
    out_shape = [shape(F32, nodes, width)]
    if weighed:
        out_specs.append(band(TALL, 1))
        out_shape.append(shape(F32, nodes, 1))
    else:
        in_specs.append(band(TALL, 1))
        args.append(inverse)
    return pl.pallas_call(
        functools.partial(near_kernel, weighed),
        grid=(nodes // TALL,),
        in_specs=in_specs,
        out_specs=out_specs,
        out_shape=out_shape,
        scratch_shapes=[pltpu.VMEM((TALL, width), BF16)],
        compiler_params=params(),
        cost_estimate=cost(),
        name="near_part",
    )(*args)


def tail_kernel(last, *refs):
    cols_ref, pos_ref, hubs_ref, tiles_ref, near_ref, weight_ref, inverse_ref = refs[:7]
    rest = refs[7:]
    if last:
        out_ref, held, wide, placed, store, averaged, sem = rest
    else:
        send_ref, out_ref, picked_ref, held, wide, placed, store, averaged, sem, total = rest
    step = pl.program_id(0)
    group = tiles_ref.shape[0]
    lanes = 4

    @pl.when(step == 0)
    def _():
        copies = []
        for owner in range(COLS):
            span = pl.ds(owner * HUB_CAP, HUB_CAP)
            copies.append(pltpu.make_async_copy(hubs_ref.at[span], held.at[span], sem.at[owner]))
        for copy in copies:
            copy.start()
        store[HUBS : HUBS + TB, :] = jnp.zeros((TB, lanes * TB), BF16)
        for owner in range(COLS):
            copies[owner].wait()
            chunk = 32

            @pl.loop(0, (pos_ref[HUBS + owner] + chunk - 1) // chunk)
            def _(n):
                top = pl.multiple_of(owner * HUB_CAP + n * chunk, chunk)
                widen(held[pl.ds(top, chunk), :].astype(F32), wide, top)

        unroll = 16

        @pl.loop(0, HUBS // unroll)
        def _(n):
            for u in range(unroll):
                slot = n * unroll + u
                move_row(wide, pos_ref[slot], placed, slot)

        for j in range(lanes):
            store[0:HUBS, j * TB : (j + 1) * TB] = placed[pl.ds(j, HUBS, stride=lanes), :].astype(BF16)

    for b in range(group):
        rights = []
        for t in range(2):
            block = cols_ref[(step * group + b) * 2 + t]
            top = jnp.where(block < 2 * ROWS, HUBS, (block - 2 * ROWS) * TB)
            rights.append(store[pl.ds(pl.multiple_of(top, TB), TB), :])
        left = jnp.concatenate([tiles_ref[b, 0], tiles_ref[b, 1]], axis=1)
        far = jnp.dot(left, jnp.concatenate(rights, axis=0), preferred_element_type=F32)
        averaged[b * TB : (b + 1) * TB, :] = (far * inverse_ref[b * TB : (b + 1) * TB, :]).astype(BF16)
    preact = near_ref[...] + jnp.dot(averaged[...], weight_ref[...], preferred_element_type=F32)
    active = jnp.maximum(preact, 0.0)
    scale = lax.rsqrt(jnp.mean(active * active, axis=1, keepdims=True) + 1e-05)
    result = (active * scale).astype(BF16)
    out_ref[...] = result
    if not last:
        add_picked(step, send_ref, result, total)

        @pl.when(step == pl.num_programs(0) - 1)
        def _():
            picked_ref[...] = total[...].astype(BF16)


def tail_part(last, cols, pos, hubs, tiles, near, weight, inverse, send=None):
    nodes, width = near.shape
    group = TALL // TB
    lanes = width // TB
    in_specs = [
        smem(),
        smem(),
        hbm(),
        band(group, 2, TB, TB),
        band(TALL, width),
        whole(width, width),
        band(TALL, 1),
    ]
    args = [cols, pos, hubs, tiles, near, weight, inverse]
    out_specs = [band(TALL, width)]
    out_shape = [shape(BF16, nodes, width)]
    scratch = [
        pltpu.VMEM(hubs.shape, BF16),
        pltpu.VMEM((hubs.shape[0] * lanes, TB), F32),
        pltpu.VMEM((HUBS * lanes, TB), F32),
        pltpu.VMEM((HUBS + TB, width), BF16),
        pltpu.VMEM((TALL, width), BF16),
        pltpu.SemaphoreType.DMA((COLS,)),
    ]
    if not last:
        in_specs.append(whole(HUB_CAP, 1))
        args.append(send)
        out_specs.append(whole(HUB_CAP, width))
        out_shape.append(shape(BF16, HUB_CAP, width))
        scratch.append(pltpu.VMEM((HUB_CAP, width), F32))
    return pl.pallas_call(
        functools.partial(tail_kernel, last),
        grid=(nodes // TALL,),
        in_specs=in_specs,
        out_specs=out_specs,
        out_shape=out_shape,
        scratch_shapes=scratch,
        compiler_params=params(),
        cost_estimate=cost(),
        name="tail_part",
    )(*args)


def send_halos(outgoing):
    width = outgoing.shape[1]
    blocks = outgoing.reshape(ROWS, -1, width)
    return lax.all_to_all(blocks, "row", 0, 0, tiled=True).reshape(-1, width)


def on_device(
    features,
    w_first,
    w_second,
    send_rows,
    halo_count,
    hub_owner,
    hub_row,
    local_cols,
    local_tiles,
    remote_cols,
    remote_tiles,
):
    width = features.shape[1]
    place = jnp.stack([lax.axis_index("row"), lax.axis_index("col")]).astype(I32)
    rows = send_rows.reshape(-1)
    count = halo_count.reshape(-1)
    cols = local_cols.reshape(-1)
    far_cols = remote_cols.reshape(-1)
    tiles, far_tiles = local_tiles[0], remote_tiles[0]
    picked, send, pos = hub_start(place, hub_owner.reshape(1, -1), hub_row, features)
    pos = pos.reshape(-1)
    gathered = lax.all_gather(picked, "col", axis=0, tiled=True)
    halos = send_halos(halo_start(True, rows, count, features))
    near, inverse = near_part(True, place, cols, far_cols, features, halos, tiles, far_tiles, w_first)
    middle, picked = tail_part(
        False, far_cols, pos, gathered, far_tiles, near, w_first[width:], inverse, send
    )
    gathered = lax.all_gather(picked, "col", axis=0, tiled=True)
    halos = send_halos(halo_start(False, rows, count, middle))
    near = near_part(False, place, cols, far_cols, middle, halos, tiles, far_tiles, w_second, inverse)[0]
    return tail_part(True, far_cols, pos, gathered, far_tiles, near, w_second[width:], inverse)[0]


def solution(mesh):
    in_specs = (
        P(("row", "col"), None),
        P(),
        P(),
        P(("row", "col"), None, None),
        P(("row", "col"), None),
        P("row", None, None),
        P("row", None),
        P(("row", "col"), None, None),
        P(("row", "col"), None, None, None, None),
        P(("row", "col"), None, None),
        P(("row", "col"), None, None, None, None),
    )
    out_specs = P(("row", "col"), None)
    return jax.shard_map(on_device, mesh=mesh, in_specs=in_specs, out_specs=out_specs, check_vma=False)
```

```python
import functools

import jax
import jax.numpy as jnp
from jax import lax
from jax.experimental import pallas as pl
from jax.experimental.pallas import tpu as pltpu
from jax.sharding import PartitionSpec as P

F32 = jnp.float32
BF16 = jnp.bfloat16
I32 = jnp.int32
MIB = 1024 * 1024
TB = 128
ROWS = 8
COLS = 16
SIDE = 4
HALO = 256
HUBS = 2048
PAIR = 24
SHARE = 128
HALF = 64
TALL = 1024


def params(mib):
    return pltpu.CompilerParams(vmem_limit_bytes=mib * MIB)


def cost():
    return pl.CostEstimate(flops=1000, bytes_accessed=1000, transcendentals=0)


def vmem():
    return pl.BlockSpec(memory_space=pltpu.VMEM)


def smem():
    return pl.BlockSpec(memory_space=pltpu.SMEM)


def hbm():
    return pl.BlockSpec(memory_space=pl.ANY)


def shape(dtype, *dims):
    return jax.ShapeDtypeStruct(dims, dtype)


def iota(dims, dim):
    return lax.broadcasted_iota(I32, dims, dim)


def widen(rows, wide, first):
    lanes = rows.shape[1] // TB
    for j in range(lanes):
        wide[pl.ds(first * lanes + j, rows.shape[0], stride=lanes), :] = rows[:, j * TB : (j + 1) * TB]


def move_row(source, row, target, slot):
    lanes = 4
    target[pl.ds(pl.multiple_of(slot * lanes, lanes), lanes), :] = source[
        pl.ds(pl.multiple_of(row * lanes, lanes), lanes), :
    ]


def write_index(my_col, owner, rows):
    my_z, my_y = my_col // SIDE, lax.rem(my_col, SIDE)
    chunks = HUBS // TB
    owner_id = iota((COLS, TB), 0)
    masks, below = [], jnp.zeros((COLS, TB), F32)
    for c in range(chunks):
        part = owner[:, c * TB : (c + 1) * TB]
        masks.append(jnp.where(part == owner_id, 1.0, 0.0))
        below = below + jnp.where(part < owner_id, 1.0, 0.0)
    offset = jnp.sum(below, axis=1, keepdims=True)
    earlier = jnp.where(iota((TB, TB), 0) < iota((TB, TB), 1), 1.0, 0.0).astype(BF16)
    inside = jnp.dot(jnp.concatenate(masks, axis=0).astype(BF16), earlier, preferred_element_type=F32)
    running = jnp.zeros((COLS, 1), F32)
    ranks, places = [], []
    for c in range(chunks):
        rank = inside[c * COLS : (c + 1) * COLS, :] + running
        ranks.append(jnp.sum(masks[c] * rank, axis=0, keepdims=True))
        places.append(jnp.sum(masks[c] * (rank + offset), axis=0, keepdims=True))
        running = running + jnp.sum(masks[c], axis=1, keepdims=True)
    rank = jnp.concatenate(ranks, axis=0).astype(I32)
    place = jnp.concatenate(places, axis=0).astype(I32)
    who = jnp.concatenate([owner[:, c * TB : (c + 1) * TB] for c in range(chunks)], axis=0)
    local = jnp.concatenate([rows[:, c * TB : (c + 1) * TB] for c in range(chunks)], axis=0).astype(F32)
    holder = lax.bitwise_and(place, COLS - 1)
    share = lax.shift_right_logical(place, 4)
    turn = lax.shift_right_logical(rank, 4)
    slot = jnp.where(who == my_col, holder * PAIR + turn, -1)
    kept = jnp.where(holder == my_col, share, -1)
    arrived = (who * PAIR + turn).astype(F32)

    def pick(keys, values, first):
        wanted = iota((TB, TB), 0) + first
        total = jnp.zeros((TB, TB), F32)
        for c in range(chunks):
            total = total + jnp.where(keys[c : c + 1, :] == wanted, values[c : c + 1, :], 0.0)
        return jnp.sum(total, axis=1, keepdims=True).astype(I32)

    send = jnp.concatenate([pick(slot, local, k * TB) for k in range(COLS * PAIR // TB)], axis=0)
    keep = pick(kept, arrived, 0)
    step_z = lax.bitwise_and(lax.shift_right_logical(holder, 2) - my_z + SIDE, SIDE - 1)
    step_y = lax.bitwise_and(lax.bitwise_and(holder, SIDE - 1) - my_y + SIDE, SIDE - 1)
    first = step_z * 256 + step_y * HALF + share
    second = HUBS // 2 + step_y * 256 + step_z * HALF + share - HALF
    return send, keep, jnp.where(share < HALF, first, second)


def choose(wanted, first, count, rows):
    chosen = jnp.where(wanted - first == iota((wanted.shape[0], count), 1), 1.0, 0.0).astype(BF16)
    return jnp.dot(chosen, rows, preferred_element_type=F32)


def load_table(table_ref, held, sem):
    chunk = held.shape[0] // SIDE
    copies = []
    for k in range(SIDE):
        span = pl.ds(k * chunk, chunk)
        copies.append(pltpu.make_async_copy(table_ref.at[span], held.at[span], sem.at[k]))
    for copy in copies:
        copy.start()
    return copies


def hub_kernel(col_ref, owner_ref, row_ref, table_ref, out_ref, send_ref, keep_ref, pos_ref, held, sem):
    copies = load_table(table_ref, held, sem)
    send, keep, pos = write_index(col_ref[0], owner_ref[...], row_ref[...])
    send_ref[...] = send
    keep_ref[...] = keep
    pos_ref[...] = pos
    chunk = held.shape[0] // SIDE
    total = jnp.zeros(out_ref.shape, F32)
    for k in range(SIDE):
        copies[k].wait()
        total = total + choose(send, k * chunk, chunk, held[k * chunk : (k + 1) * chunk, :])
    out_ref[...] = total.astype(BF16)


def hub_start(my_col, owner, rows, table):
    nodes, width = table.shape
    sent = COLS * PAIR
    return pl.pallas_call(
        hub_kernel,
        in_specs=[smem(), vmem(), vmem(), hbm()],
        out_specs=[vmem()] * 4,
        out_shape=[shape(BF16, sent, width), shape(I32, sent, 1), shape(I32, SHARE, 1), shape(I32, HUBS // TB, TB)],
        scratch_shapes=[pltpu.VMEM((nodes, width), BF16), pltpu.SemaphoreType.DMA((SIDE,))],
        compiler_params=params(60),
        cost_estimate=cost(),
        name="hub_start",
    )(my_col, owner, rows, table)


def keep_kernel(keep_ref, arrived_ref, first_ref, second_ref):
    kept = choose(keep_ref[...], 0, arrived_ref.shape[0], arrived_ref[...]).astype(BF16)
    first_ref[...] = kept[:HALF]
    second_ref[...] = kept[HALF:]


def hub_keep(keep_index, arrived):
    half = shape(BF16, HALF, arrived.shape[1])
    return pl.pallas_call(
        keep_kernel,
        in_specs=[vmem(), vmem()],
        out_specs=[vmem(), vmem()],
        out_shape=[half, half],
        compiler_params=params(60),
        cost_estimate=cost(),
        name="hub_keep",
    )(keep_index, arrived)


def halo_kernel(rows_ref, count_ref, table_ref, out_ref, held, wide, picked, staged, sem, out_sem):
    lanes = 4
    unroll = 32
    copies = load_table(table_ref, held, sem)
    chunk = held.shape[0] // SIDE
    for k in range(SIDE):
        copies[k].wait()

        @pl.loop(0, chunk // TB)
        def _(n):
            top = pl.multiple_of(k * chunk + n * TB, TB)
            widen(held[pl.ds(top, TB), :].astype(F32), wide, top)

    out = [
        pltpu.make_async_copy(
            staged.at[pl.ds(peer * HALO, HALO)], out_ref.at[pl.ds(peer * HALO, HALO)], out_sem.at[peer]
        )
        for peer in range(ROWS)
    ]
    for peer in range(ROWS):
        count = count_ref[0, peer]

        @pl.loop(0, (count + unroll - 1) // unroll)
        def _(group):
            for u in range(unroll):
                slot = group * unroll + u
                move_row(wide, rows_ref[peer, slot], picked, slot)

        for half in range(HALO // TB):
            live = iota((TB, TB), 0) + half * TB < count
            top = peer * HALO + half * TB
            for j in range(lanes):
                part = picked[pl.ds(half * TB * lanes + j, TB, stride=lanes), :]
                staged[top : top + TB, j * TB : (j + 1) * TB] = jnp.where(live, part, 0.0).astype(BF16)
        out[peer].start()
    for copy in out:
        copy.wait()


def halo_start(rows, count, table):
    nodes, width = table.shape
    lanes = width // TB
    return pl.pallas_call(
        halo_kernel,
        in_specs=[smem(), smem(), hbm()],
        out_specs=hbm(),
        out_shape=shape(BF16, ROWS * HALO, width),
        scratch_shapes=[
            pltpu.VMEM((nodes, width), BF16),
            pltpu.VMEM((nodes * lanes, TB), F32),
            pltpu.VMEM((HALO * lanes, TB), F32),
            pltpu.VMEM((ROWS * HALO, width), BF16),
            pltpu.SemaphoreType.DMA((SIDE,)),
            pltpu.SemaphoreType.DMA((ROWS,)),
        ],
        compiler_params=params(60),
        cost_estimate=cost(),
        name="halo_start",
    )(rows, count, table)


def start_chunks(pairs, sem):
    copies = [pltpu.make_async_copy(source, target, sem.at[k]) for k, (source, target) in enumerate(pairs)]
    for copy in copies:
        copy.start()
    return copies


def chunk_copies(source, target, sem):
    return [
        pltpu.make_async_copy(source.at[pl.ds(k * TALL, TALL)], target.at[pl.ds(k * TALL, TALL)], sem.at[k])
        for k in range(source.shape[0] // TALL)
    ]


def gather_blocks(table, cols_ref, block):
    tops = [pl.multiple_of(cols_ref[t, block] * TB, TB) for t in range(2)]
    return jnp.concatenate([table[pl.ds(top, TB), :] for top in tops], axis=0)


def tail_kernel(last, *refs):
    pieces = refs[:8]
    row_ref, count_ref, cols_ref, far_ref, pos_ref = refs[8:13]
    halo_ref, table_ref, tiles_ref, far_tiles_ref, weight_ref = refs[13:18]
    rest = refs[18:]
    if last:
        out_ref = rest[0]
        rest = rest[1:]
    else:
        send_ref, out_ref, picked_ref, total = rest[:3] + rest[-1:]
        rest = rest[3:-1]
    held, wide, placed, store, table, tiles, far_tiles, weight, joined, result, sem, out_sem = rest
    lanes = 4
    size = HUBS // 8
    width = store.shape[1]
    halo_rows = ROWS * HALO
    pairs = [(pieces[k], held.at[pl.ds(k * size, size)]) for k in range(8)]
    pairs.append((table_ref, table))
    pairs.append((weight_ref, weight))
    pairs.append((tiles_ref, tiles))
    pairs.append((halo_ref, store.at[pl.ds(0, halo_rows)]))
    pairs.append((far_tiles_ref, far_tiles))
    copies = start_chunks(pairs, sem)
    for k in range(8):
        copies[k].wait()
        widen(held[k * size : (k + 1) * size, :].astype(F32), wide, k * size)
    unroll = 64
    for k in range(HUBS // TB):

        @pl.loop(0, TB // unroll)
        def _(n):
            for u in range(unroll):
                slot = n * unroll + u
                move_row(wide, pos_ref[k, slot], placed, k * TB + slot)

    for j in range(lanes):
        store[halo_rows : halo_rows + HUBS, j * TB : (j + 1) * TB] = placed[pl.ds(j, HUBS, stride=lanes), :].astype(BF16)
    for copy in copies[8:]:
        copy.wait()
    out = chunk_copies(result, out_ref, out_sem)
    group = TALL // TB
    my_row = row_ref[0]
    for k in range(result.shape[0] // TALL):
        for b in range(group):
            block = k * group + b
            near, far = tiles[block], far_tiles[block]
            left = jnp.concatenate([near[0], near[1], far[0], far[1]], axis=1)
            right = jnp.concatenate([gather_blocks(table, cols_ref, block), gather_blocks(store, far_ref, block)], axis=0)
            total_rows = jnp.dot(left, right, preferred_element_type=F32)
            mass = near[0].astype(F32) + near[1].astype(F32)
            for t in range(2):
                col = far_ref[t, block]
                peer = lax.bitwise_and(lax.shift_right_logical(col, 1), ROWS - 1)
                count = count_ref[lax.bitwise_xor(peer, my_row), my_row]
                live = jnp.where(col < 2 * ROWS, count - lax.bitwise_and(col, 1) * TB, TB)
                mass = mass + jnp.where(iota((TB, TB), 1) < live, far[t].astype(F32), 0.0)
            inverse = 1.0 / jnp.sum(mass, axis=1, keepdims=True)
            joined[b * TB : (b + 1) * TB, width : 2 * width] = (total_rows * inverse).astype(BF16)
        span = slice(k * TALL, (k + 1) * TALL)
        joined[:, 0:width] = table[span, :]
        preact = jnp.dot(joined[...], weight[...], preferred_element_type=F32)
        active = jnp.maximum(preact, 0.0)
        scale = lax.rsqrt(jnp.mean(active * active, axis=1, keepdims=True) + 1e-05)
        rows = (active * scale).astype(BF16)
        result[span, :] = rows
        out[k].start()
        if not last:
            part = choose(send_ref[...], k * TALL, TALL, rows)
            if k == 0:
                total[...] = part
            else:
                total[...] = total[...] + part
    if not last:
        picked_ref[...] = total[...].astype(BF16)
    for copy in out:
        copy.wait()


def tail_part(last, hubs, row, count, cols, far_cols, pos, halos, table, tiles, far_tiles, weight, send=None):
    nodes, width = table.shape
    lanes = width // TB
    in_specs = [hbm()] * 8 + [smem()] * 5 + [hbm()] * 5
    args = [*hubs, row, count, cols, far_cols, pos, halos, table, tiles, far_tiles, weight]
    out_specs = [hbm()]
    out_shape = [shape(BF16, nodes, width)]
    scratch = [
        pltpu.VMEM((HUBS, width), BF16),
        pltpu.VMEM((HUBS * lanes, TB), F32),
        pltpu.VMEM((HUBS * lanes, TB), F32),
        pltpu.VMEM((ROWS * HALO + HUBS, width), BF16),
        pltpu.VMEM((nodes, width), BF16),
        pltpu.VMEM(tiles.shape, BF16),
        pltpu.VMEM(far_tiles.shape, BF16),
        pltpu.VMEM(weight.shape, BF16),
        pltpu.VMEM((TALL, 2 * width), BF16),
        pltpu.VMEM((nodes, width), BF16),
        pltpu.SemaphoreType.DMA((13,)),
        pltpu.SemaphoreType.DMA((nodes // TALL,)),
    ]
    if not last:
        sent = COLS * PAIR
        in_specs.append(vmem())
        args.append(send)
        out_specs.append(vmem())
        out_shape.append(shape(BF16, sent, width))
        scratch.append(pltpu.VMEM((sent, width), F32))
    return pl.pallas_call(
        functools.partial(tail_kernel, last),
        in_specs=in_specs,
        out_specs=out_specs,
        out_shape=out_shape,
        scratch_shapes=scratch,
        compiler_params=params(60),
        cost_estimate=cost(),
        name="tail_part",
    )(*args)


def fetch(array, dz, dy):
    pairs = [
        (((z + dz) % SIDE) * SIDE + (y + dy) % SIDE, z * SIDE + y) for z in range(SIDE) for y in range(SIDE)
    ]
    return lax.ppermute(array, "col", pairs)


def spread_hubs(first, second):
    order = (1, 3, 2)
    near_y = {k: fetch(first, 0, k) for k in order}
    near_z = {k: fetch(second, k, 0) for k in order}
    first_all = jnp.concatenate([first] + [near_y[k] for k in range(1, SIDE)], axis=0)
    second_all = jnp.concatenate([second] + [near_z[k] for k in range(1, SIDE)], axis=0)
    far_z = {k: fetch(first_all, k, 0) for k in order}
    far_y = {k: fetch(second_all, 0, k) for k in order}
    left = [first_all] + [far_z[k] for k in range(1, SIDE)]
    right = [second_all] + [far_y[k] for k in range(1, SIDE)]
    return left + right


def share_counts(count):
    table = count
    for bit in (1, 2, 4):
        pairs = [(i, i ^ bit) for i in range(ROWS)]
        table = jnp.concatenate([table, lax.ppermute(table, "row", pairs)], axis=0)
    return table


def exchange(picked, keep, outgoing):
    width = picked.shape[1]
    arrived = lax.all_to_all(picked.reshape(COLS, PAIR, width), "col", 0, 0, tiled=True)
    arrived, outgoing = lax.optimization_barrier((arrived.reshape(-1, width), outgoing))
    hubs = spread_hubs(*hub_keep(keep, arrived))
    halos = lax.all_to_all(outgoing.reshape(ROWS, HALO, width), "row", 0, 0, tiled=True)
    return hubs, halos.reshape(-1, width)


def on_device(
    features,
    w_first,
    w_second,
    send_rows,
    halo_count,
    hub_owner,
    hub_row,
    local_cols,
    local_tiles,
    remote_cols,
    remote_tiles,
):
    my_row = lax.axis_index("row").astype(I32).reshape(1)
    my_col = lax.axis_index("col").astype(I32).reshape(1)
    rows = send_rows[0]
    cols = local_cols[0].T
    far_cols = remote_cols[0].T
    tiles, far_tiles = local_tiles[0], remote_tiles[0]
    counts = share_counts(halo_count)
    picked, send, keep, pos = hub_start(my_col, hub_owner.reshape(1, -1), hub_row, features)
    outgoing, counts = lax.optimization_barrier((halo_start(rows, halo_count, features), counts))
    hubs, halos = exchange(picked, keep, outgoing)
    shared = (my_row, counts, cols, far_cols, pos)
    middle, picked = tail_part(False, hubs, *shared, halos, features, tiles, far_tiles, w_first, send)
    hubs, halos = exchange(picked, keep, halo_start(rows, halo_count, middle))
    return tail_part(True, hubs, *shared, halos, middle, tiles, far_tiles, w_second)[0]


def solution(mesh):
    in_specs = (
        P(("row", "col"), None),
        P(),
        P(),
        P(("row", "col"), None, None),
        P(("row", "col"), None),
        P("row", None, None),
        P("row", None),
        P(("row", "col"), None, None),
        P(("row", "col"), None, None, None, None),
        P(("row", "col"), None, None),
        P(("row", "col"), None, None, None, None),
    )
    out_specs = P(("row", "col"), None)
    return jax.shard_map(on_device, mesh=mesh, in_specs=in_specs, out_specs=out_specs, check_vma=False)
```

```python
import functools

import jax
import jax.numpy as jnp
from jax import lax
from jax.experimental import pallas as pl
from jax.experimental.pallas import tpu as pltpu
from jax.sharding import PartitionSpec as P

F32 = jnp.float32
BF16 = jnp.bfloat16
I32 = jnp.int32
MIB = 1024 * 1024
TB = 128
ROWS = 8
COLS = 16
SIDE = 4
HALO = 256
NOTE = 16
HUBS = 2048
PAIR = 24
SHARE = 128
HALF = 64
TALL = 1024


def params(mib):
    return pltpu.CompilerParams(vmem_limit_bytes=mib * MIB)


def cost():
    return pl.CostEstimate(flops=1000, bytes_accessed=1000, transcendentals=0)


def vmem():
    return pl.BlockSpec(memory_space=pltpu.VMEM)


def smem():
    return pl.BlockSpec(memory_space=pltpu.SMEM)


def hbm():
    return pl.BlockSpec(memory_space=pl.ANY)


def shape(dtype, *dims):
    return jax.ShapeDtypeStruct(dims, dtype)


def iota(dims, dim):
    return lax.broadcasted_iota(I32, dims, dim)


def widen(rows, wide, first):
    lanes = rows.shape[1] // TB
    for j in range(lanes):
        wide[pl.ds(first * lanes + j, rows.shape[0], stride=lanes), :] = rows[:, j * TB : (j + 1) * TB]


def move_row(source, row, target, slot):
    lanes = 4
    target[pl.ds(pl.multiple_of(slot * lanes, lanes), lanes), :] = source[
        pl.ds(pl.multiple_of(row * lanes, lanes), lanes), :
    ]


def write_index(my_col, owner, rows):
    my_z, my_y = my_col // SIDE, lax.rem(my_col, SIDE)
    chunks = HUBS // TB
    owner_id = iota((COLS, TB), 0)
    masks, below = [], jnp.zeros((COLS, TB), F32)
    for c in range(chunks):
        part = owner[:, c * TB : (c + 1) * TB]
        masks.append(jnp.where(part == owner_id, 1.0, 0.0))
        below = below + jnp.where(part < owner_id, 1.0, 0.0)
    offset = jnp.sum(below, axis=1, keepdims=True)
    earlier = jnp.where(iota((TB, TB), 0) < iota((TB, TB), 1), 1.0, 0.0).astype(BF16)
    inside = jnp.dot(jnp.concatenate(masks, axis=0).astype(BF16), earlier, preferred_element_type=F32)
    running = jnp.zeros((COLS, 1), F32)
    ranks, places = [], []
    for c in range(chunks):
        rank = inside[c * COLS : (c + 1) * COLS, :] + running
        ranks.append(jnp.sum(masks[c] * rank, axis=0, keepdims=True))
        places.append(jnp.sum(masks[c] * (rank + offset), axis=0, keepdims=True))
        running = running + jnp.sum(masks[c], axis=1, keepdims=True)
    rank = jnp.concatenate(ranks, axis=0).astype(I32)
    place = jnp.concatenate(places, axis=0).astype(I32)
    who = jnp.concatenate([owner[:, c * TB : (c + 1) * TB] for c in range(chunks)], axis=0)
    local = jnp.concatenate([rows[:, c * TB : (c + 1) * TB] for c in range(chunks)], axis=0).astype(F32)
    holder = lax.bitwise_and(place, COLS - 1)
    share = lax.shift_right_logical(place, 4)
    turn = lax.shift_right_logical(rank, 4)
    slot = jnp.where(who == my_col, holder * PAIR + turn, -1)
    kept = jnp.where(holder == my_col, share, -1)
    arrived = (who * PAIR + turn).astype(F32)

    def pick(keys, values, first):
        wanted = iota((TB, TB), 0) + first
        total = jnp.zeros((TB, TB), F32)
        for c in range(chunks):
            total = total + jnp.where(keys[c : c + 1, :] == wanted, values[c : c + 1, :], 0.0)
        return jnp.sum(total, axis=1, keepdims=True).astype(I32)

    send = jnp.concatenate([pick(slot, local, k * TB) for k in range(COLS * PAIR // TB)], axis=0)
    keep = pick(kept, arrived, 0)
    step_z = lax.bitwise_and(lax.shift_right_logical(holder, 2) - my_z + SIDE, SIDE - 1)
    step_y = lax.bitwise_and(lax.bitwise_and(holder, SIDE - 1) - my_y + SIDE, SIDE - 1)
    first = step_z * 256 + step_y * HALF + share
    second = HUBS // 2 + step_y * 256 + step_z * HALF + share - HALF
    return send, keep, jnp.where(share < HALF, first, second)


def choose(wanted, first, count, rows):
    chosen = jnp.where(wanted - first == iota((wanted.shape[0], count), 1), 1.0, 0.0).astype(BF16)
    return jnp.dot(chosen, rows, preferred_element_type=F32)


def load_table(table_ref, held, sem):
    chunk = held.shape[0] // SIDE
    copies = []
    for k in range(SIDE):
        span = pl.ds(k * chunk, chunk)
        copies.append(pltpu.make_async_copy(table_ref.at[span], held.at[span], sem.at[k]))
    for copy in copies:
        copy.start()
    return copies


def hub_kernel(col_ref, owner_ref, row_ref, table_ref, out_ref, send_ref, keep_ref, pos_ref, held, sem):
    copies = load_table(table_ref, held, sem)
    send, keep, pos = write_index(col_ref[0], owner_ref[...], row_ref[...])
    send_ref[...] = send
    keep_ref[...] = keep
    pos_ref[...] = pos
    chunk = held.shape[0] // SIDE
    total = jnp.zeros(out_ref.shape, F32)
    for k in range(SIDE):
        copies[k].wait()
        total = total + choose(send, k * chunk, chunk, held[k * chunk : (k + 1) * chunk, :])
    out_ref[...] = total.astype(BF16)


def hub_start(my_col, owner, rows, table):
    nodes, width = table.shape
    sent = COLS * PAIR
    return pl.pallas_call(
        hub_kernel,
        in_specs=[smem(), vmem(), vmem(), hbm()],
        out_specs=[vmem()] * 4,
        out_shape=[shape(BF16, sent, width), shape(I32, sent, 1), shape(I32, SHARE, 1), shape(I32, HUBS // TB, TB)],
        scratch_shapes=[pltpu.VMEM((nodes, width), BF16), pltpu.SemaphoreType.DMA((SIDE,))],
        compiler_params=params(60),
        cost_estimate=cost(),
        name="hub_start",
    )(my_col, owner, rows, table)


def keep_kernel(keep_ref, arrived_ref, first_ref, second_ref):
    kept = choose(keep_ref[...], 0, arrived_ref.shape[0], arrived_ref[...]).astype(BF16)
    first_ref[...] = kept[:HALF]
    second_ref[...] = kept[HALF:]


def hub_keep(keep_index, arrived):
    half = shape(BF16, HALF, arrived.shape[1])
    return pl.pallas_call(
        keep_kernel,
        in_specs=[vmem(), vmem()],
        out_specs=[vmem(), vmem()],
        out_shape=[half, half],
        compiler_params=params(8),
        cost_estimate=cost(),
        name="hub_keep",
    )(keep_index, arrived)


def halo_kernel(noted, rows_ref, count_ref, table_ref, out_ref, held, wide, picked, staged, sem, out_sem):
    lanes = 4
    unroll = 32
    height = HALO + (NOTE if noted else 0)
    copies = load_table(table_ref, held, sem)
    chunk = held.shape[0] // SIDE
    for k in range(SIDE):
        copies[k].wait()

        @pl.loop(0, chunk // TB)
        def _(n):
            top = pl.multiple_of(k * chunk + n * TB, TB)
            widen(held[pl.ds(top, TB), :].astype(F32), wide, top)

    out = [
        pltpu.make_async_copy(
            staged.at[pl.ds(peer * height, height)], out_ref.at[pl.ds(peer * height, height)], out_sem.at[peer]
        )
        for peer in range(ROWS)
    ]
    for peer in range(ROWS):
        count = count_ref[0, peer]

        @pl.loop(0, (count + unroll - 1) // unroll)
        def _(group):
            for u in range(unroll):
                slot = group * unroll + u
                move_row(wide, rows_ref[peer * HALO + slot], picked, slot)

        for half in range(HALO // TB):
            live = iota((TB, TB), 0) + half * TB < count
            top = peer * height + half * TB
            for j in range(lanes):
                part = picked[pl.ds(half * TB * lanes + j, TB, stride=lanes), :]
                staged[top : top + TB, j * TB : (j + 1) * TB] = jnp.where(live, part, 0.0).astype(BF16)
        if noted:
            top = peer * height + HALO
            staged[top : top + NOTE, :] = jnp.full((NOTE, lanes * TB), count, I32).astype(F32).astype(BF16)
        out[peer].start()
    for copy in out:
        copy.wait()


def halo_start(noted, rows, count, table):
    nodes, width = table.shape
    height = ROWS * (HALO + (NOTE if noted else 0))
    lanes = width // TB
    return pl.pallas_call(
        functools.partial(halo_kernel, noted),
        in_specs=[smem(), smem(), hbm()],
        out_specs=hbm(),
        out_shape=shape(BF16, height, width),
        scratch_shapes=[
            pltpu.VMEM((nodes, width), BF16),
            pltpu.VMEM((nodes * lanes, TB), F32),
            pltpu.VMEM((HALO * lanes, TB), F32),
            pltpu.VMEM((height, width), BF16),
            pltpu.SemaphoreType.DMA((SIDE,)),
            pltpu.SemaphoreType.DMA((ROWS,)),
        ],
        compiler_params=params(60),
        cost_estimate=cost(),
        name="halo_start",
    )(rows, count, table)


def start_chunks(pairs, sem):
    copies = [pltpu.make_async_copy(source, target, sem.at[k]) for k, (source, target) in enumerate(pairs)]
    for copy in copies:
        copy.start()
    return copies


def chunk_copies(source, target, sem):
    return [
        pltpu.make_async_copy(source.at[pl.ds(k * TALL, TALL)], target.at[pl.ds(k * TALL, TALL)], sem.at[k])
        for k in range(source.shape[0] // TALL)
    ]


def gather_blocks(table, cols_ref, block):
    tops = [pl.multiple_of(cols_ref[t, block] * TB, TB) for t in range(2)]
    return jnp.concatenate([table[pl.ds(top, TB), :] for top in tops], axis=0)


def tail_kernel(last, *refs):
    pieces = refs[:8]
    cols_ref, far_ref, pos_ref, halo_ref, table_ref, tiles_ref, far_tiles_ref, weight_ref = refs[8:16]
    rest = refs[16:]
    if last:
        counts, out_ref = rest[:2]
        rest = rest[2:]
    else:
        send_ref, out_ref, picked_ref, counts = rest[:4]
        notes, total = rest[-2:]
        rest = rest[4:-2]
    held, wide, placed, store, table, tiles, far_tiles, weight, joined, result, sem, out_sem = rest
    lanes = 4
    size = HUBS // 8
    width = store.shape[1]
    halo_rows = ROWS * HALO
    height = halo_ref.shape[0] // ROWS
    pairs = [(pieces[k], held.at[pl.ds(k * size, size)]) for k in range(8)]
    pairs += [(table_ref, table), (tiles_ref, tiles), (far_tiles_ref, far_tiles)]
    for p in range(ROWS):
        pairs.append((halo_ref.at[pl.ds(p * height, HALO)], store.at[pl.ds(p * HALO, HALO)]))
        if not last:
            pairs.append((halo_ref.at[pl.ds(p * height + HALO, NOTE)], notes.at[pl.ds(p * NOTE, NOTE)]))
    pairs.append((weight_ref, weight))
    copies = start_chunks(pairs, sem)
    for k in range(8):
        copies[k].wait()
        widen(held[k * size : (k + 1) * size, :].astype(F32), wide, k * size)
    unroll = 64
    for k in range(HUBS // TB):

        @pl.loop(0, TB // unroll)
        def _(n):
            for u in range(unroll):
                slot = n * unroll + u
                move_row(wide, pos_ref[k, slot], placed, k * TB + slot)

    for j in range(lanes):
        store[halo_rows : halo_rows + HUBS, j * TB : (j + 1) * TB] = placed[pl.ds(j, HUBS, stride=lanes), :].astype(BF16)
    for copy in copies[8:]:
        copy.wait()
    if not last:
        for p in range(ROWS):
            counts[p : p + 1, :] = notes[p * NOTE : (p + 1) * NOTE, 0:TB].astype(F32)[0:1, :]
        counts[ROWS : 2 * ROWS, :] = jnp.full((ROWS, TB), 1024.0, F32)
    out = chunk_copies(result, out_ref, out_sem)
    group = TALL // TB
    for k in range(result.shape[0] // TALL):
        for b in range(group):
            block = k * group + b
            near, far = tiles[block], far_tiles[block]
            left = jnp.concatenate([near[0], near[1], far[0], far[1]], axis=1)
            right = jnp.concatenate([gather_blocks(table, cols_ref, block), gather_blocks(store, far_ref, block)], axis=0)
            total_rows = jnp.dot(left, right, preferred_element_type=F32)
            mass = near[0].astype(F32) + near[1].astype(F32)
            for t in range(2):
                col = far_ref[t, block]
                peer = jnp.minimum(lax.shift_right_logical(col, 1), ROWS)
                slots = (iota((1, TB), 1) + lax.bitwise_and(col, 1) * TB).astype(F32)
                mass = mass + jnp.where(slots < counts[pl.ds(peer, 1), :], far[t].astype(F32), 0.0)
            inverse = 1.0 / jnp.sum(mass, axis=1, keepdims=True)
            joined[b * TB : (b + 1) * TB, width : 2 * width] = (total_rows * inverse).astype(BF16)
        span = slice(k * TALL, (k + 1) * TALL)
        joined[:, 0:width] = table[span, :]
        preact = jnp.dot(joined[...], weight[...], preferred_element_type=F32)
        active = jnp.maximum(preact, 0.0)
        scale = lax.rsqrt(jnp.mean(active * active, axis=1, keepdims=True) + 1e-05)
        rows = (active * scale).astype(BF16)
        result[span, :] = rows
        out[k].start()
        if not last:
            part = choose(send_ref[...], k * TALL, TALL, rows)
            if k == 0:
                total[...] = part
            else:
                total[...] = total[...] + part
    if not last:
        picked_ref[...] = total[...].astype(BF16)
    for copy in out:
        copy.wait()


def tail_part(last, hubs, cols, far_cols, pos, halos, table, tiles, far_tiles, weight, extra):
    nodes, width = table.shape
    lanes = width // TB
    in_specs = [hbm()] * 8 + [smem()] * 3 + [hbm()] * 5 + [vmem()]
    args = [*hubs, cols, far_cols, pos, halos, table, tiles, far_tiles, weight, extra]
    out_specs = [hbm()]
    out_shape = [shape(BF16, nodes, width)]
    scratch = [
        pltpu.VMEM((HUBS, width), BF16),
        pltpu.VMEM((HUBS * lanes, TB), F32),
        pltpu.VMEM((HUBS * lanes, TB), F32),
        pltpu.VMEM((ROWS * HALO + HUBS, width), BF16),
        pltpu.VMEM((nodes, width), BF16),
        pltpu.VMEM(tiles.shape, BF16),
        pltpu.VMEM(far_tiles.shape, BF16),
        pltpu.VMEM(weight.shape, BF16),
        pltpu.VMEM((TALL, 2 * width), BF16),
        pltpu.VMEM((nodes, width), BF16),
        pltpu.SemaphoreType.DMA((32,)),
        pltpu.SemaphoreType.DMA((nodes // TALL,)),
    ]
    if not last:
        sent = COLS * PAIR
        out_specs += [vmem(), vmem()]
        out_shape += [shape(BF16, sent, width), shape(F32, 2 * ROWS, TB)]
        scratch += [pltpu.VMEM((ROWS * NOTE, width), BF16), pltpu.VMEM((sent, width), F32)]
    return pl.pallas_call(
        functools.partial(tail_kernel, last),
        in_specs=in_specs,
        out_specs=out_specs,
        out_shape=out_shape,
        scratch_shapes=scratch,
        compiler_params=params(54),
        cost_estimate=cost(),
        name="tail_part",
    )(*args)


def fetch(array, dz, dy):
    pairs = [
        (((z + dz) % SIDE) * SIDE + (y + dy) % SIDE, z * SIDE + y) for z in range(SIDE) for y in range(SIDE)
    ]
    return lax.ppermute(array, "col", pairs)


def spread_hubs(first, second):
    order = (1, 3, 2)
    near_y = {k: fetch(first, 0, k) for k in order}
    near_z = {k: fetch(second, k, 0) for k in order}
    first_all = jnp.concatenate([first] + [near_y[k] for k in range(1, SIDE)], axis=0)
    second_all = jnp.concatenate([second] + [near_z[k] for k in range(1, SIDE)], axis=0)
    far_z = {k: fetch(first_all, k, 0) for k in order}
    far_y = {k: fetch(second_all, 0, k) for k in order}
    left = [first_all] + [far_z[k] for k in range(1, SIDE)]
    right = [second_all] + [far_y[k] for k in range(1, SIDE)]
    return left + right


def exchange(picked, keep, outgoing):
    width = picked.shape[1]
    arrived = lax.all_to_all(picked.reshape(COLS, PAIR, width), "col", 0, 0, tiled=True)
    arrived, outgoing = lax.optimization_barrier((arrived.reshape(-1, width), outgoing))
    hubs = spread_hubs(*hub_keep(keep, arrived))
    halos = lax.all_to_all(outgoing.reshape(ROWS, -1, width), "row", 0, 0, tiled=True)
    return hubs, halos.reshape(-1, width)


def on_device(
    features,
    w_first,
    w_second,
    send_rows,
    halo_count,
    hub_owner,
    hub_row,
    local_cols,
    local_tiles,
    remote_cols,
    remote_tiles,
):
    my_col = lax.axis_index("col").astype(I32).reshape(1)
    rows = send_rows.reshape(-1)
    cols = local_cols[0].T
    far_cols = remote_cols[0].T
    tiles, far_tiles = local_tiles[0], remote_tiles[0]
    picked, send, keep, pos = hub_start(my_col, hub_owner.reshape(1, -1), hub_row, features)
    hubs, halos = exchange(picked, keep, halo_start(True, rows, halo_count, features))
    middle, picked, counts = tail_part(
        False, hubs, cols, far_cols, pos, halos, features, tiles, far_tiles, w_first, send
    )
    hubs, halos = exchange(picked, keep, halo_start(False, rows, halo_count, middle))
    return tail_part(True, hubs, cols, far_cols, pos, halos, middle, tiles, far_tiles, w_second, counts)[0]


def solution(mesh):
    in_specs = (
        P(("row", "col"), None),
        P(),
        P(),
        P(("row", "col"), None, None),
        P(("row", "col"), None),
        P("row", None, None),
        P("row", None),
        P(("row", "col"), None, None),
        P(("row", "col"), None, None, None, None),
        P(("row", "col"), None, None),
        P(("row", "col"), None, None, None, None),
    )
    out_specs = P(("row", "col"), None)
    return jax.shard_map(on_device, mesh=mesh, in_specs=in_specs, out_specs=out_specs, check_vma=False)
```

```python
import functools

import jax
import jax.numpy as jnp
from jax import lax
from jax.experimental import pallas as pl
from jax.experimental.pallas import tpu as pltpu
from jax.sharding import PartitionSpec as P

F32 = jnp.float32
BF16 = jnp.bfloat16
I32 = jnp.int32
MIB = 1024 * 1024
TB = 128
ROWS = 8
COLS = 16
SIDE = 4
HALO = 256
NOTE = 16
HUBS = 2048
PAIR = 24
SHARE = 128
HALF = 64
TALL = 1024


def params(mib):
    return pltpu.CompilerParams(vmem_limit_bytes=mib * MIB)


def cost():
    return pl.CostEstimate(flops=1000, bytes_accessed=1000, transcendentals=0)


def vmem():
    return pl.BlockSpec(memory_space=pltpu.VMEM)


def smem():
    return pl.BlockSpec(memory_space=pltpu.SMEM)


def hbm():
    return pl.BlockSpec(memory_space=pl.ANY)


def shape(dtype, *dims):
    return jax.ShapeDtypeStruct(dims, dtype)


def iota(dims, dim):
    return lax.broadcasted_iota(I32, dims, dim)


def widen(rows, wide, first):
    lanes = rows.shape[1] // TB
    for j in range(lanes):
        wide[pl.ds(first * lanes + j, rows.shape[0], stride=lanes), :] = rows[:, j * TB : (j + 1) * TB]


def move_row(source, row, target, slot):
    lanes = 4
    target[pl.ds(pl.multiple_of(slot * lanes, lanes), lanes), :] = source[
        pl.ds(pl.multiple_of(row * lanes, lanes), lanes), :
    ]


def write_index(my_col, owner, rows):
    my_z, my_y = my_col // SIDE, lax.rem(my_col, SIDE)
    chunks = HUBS // TB
    owner_id = iota((COLS, TB), 0)
    masks, below = [], jnp.zeros((COLS, TB), F32)
    for c in range(chunks):
        part = owner[:, c * TB : (c + 1) * TB]
        masks.append(jnp.where(part == owner_id, 1.0, 0.0))
        below = below + jnp.where(part < owner_id, 1.0, 0.0)
    offset = jnp.sum(below, axis=1, keepdims=True)
    earlier = jnp.where(iota((TB, TB), 0) < iota((TB, TB), 1), 1.0, 0.0).astype(BF16)
    inside = jnp.dot(jnp.concatenate(masks, axis=0).astype(BF16), earlier, preferred_element_type=F32)
    running = jnp.zeros((COLS, 1), F32)
    ranks, places = [], []
    for c in range(chunks):
        rank = inside[c * COLS : (c + 1) * COLS, :] + running
        ranks.append(jnp.sum(masks[c] * rank, axis=0, keepdims=True))
        places.append(jnp.sum(masks[c] * (rank + offset), axis=0, keepdims=True))
        running = running + jnp.sum(masks[c], axis=1, keepdims=True)
    rank = jnp.concatenate(ranks, axis=0).astype(I32)
    place = jnp.concatenate(places, axis=0).astype(I32)
    who = jnp.concatenate([owner[:, c * TB : (c + 1) * TB] for c in range(chunks)], axis=0)
    local = jnp.concatenate([rows[:, c * TB : (c + 1) * TB] for c in range(chunks)], axis=0).astype(F32)
    holder = lax.bitwise_and(place, COLS - 1)
    share = lax.shift_right_logical(place, 4)
    turn = lax.shift_right_logical(rank, 4)
    slot = jnp.where(who == my_col, holder * PAIR + turn, -1)
    kept = jnp.where(holder == my_col, share, -1)
    arrived = (who * PAIR + turn).astype(F32)

    def pick(keys, values, first):
        wanted = iota((TB, TB), 0) + first
        total = jnp.zeros((TB, TB), F32)
        for c in range(chunks):
            total = total + jnp.where(keys[c : c + 1, :] == wanted, values[c : c + 1, :], 0.0)
        return jnp.sum(total, axis=1, keepdims=True).astype(I32)

    send = jnp.concatenate([pick(slot, local, k * TB) for k in range(COLS * PAIR // TB)], axis=0)
    keep = pick(kept, arrived, 0)
    step_z = lax.bitwise_and(lax.shift_right_logical(holder, 2) - my_z + SIDE, SIDE - 1)
    step_y = lax.bitwise_and(lax.bitwise_and(holder, SIDE - 1) - my_y + SIDE, SIDE - 1)
    first = step_z * 256 + step_y * HALF + share
    second = HUBS // 2 + step_y * 256 + step_z * HALF + share - HALF
    return send, keep, jnp.where(share < HALF, first, second)


def choose(wanted, first, count, rows):
    chosen = jnp.where(wanted - first == iota((wanted.shape[0], count), 1), 1.0, 0.0).astype(BF16)
    return jnp.dot(chosen, rows, preferred_element_type=F32)


def load_table(table_ref, held, sem):
    chunk = held.shape[0] // SIDE
    copies = []
    for k in range(SIDE):
        span = pl.ds(k * chunk, chunk)
        copies.append(pltpu.make_async_copy(table_ref.at[span], held.at[span], sem.at[k]))
    for copy in copies:
        copy.start()
    return copies


def hub_kernel(col_ref, owner_ref, row_ref, table_ref, out_ref, send_ref, keep_ref, pos_ref, held, sem):
    copies = load_table(table_ref, held, sem)
    send, keep, pos = write_index(col_ref[0], owner_ref[...], row_ref[...])
    lists = SIDE - 1
    parts = [send[k * TB : (k + 1) * TB, :].astype(F32) for k in range(lists)]
    square = jnp.concatenate(parts + [jnp.zeros((TB, TB - lists), F32)], axis=1)
    send_ref[...] = square.T[0:8, :].astype(I32)
    keep_ref[...] = keep
    pos_ref[...] = pos
    chunk = held.shape[0] // SIDE
    total = jnp.zeros(out_ref.shape, F32)
    for k in range(SIDE):
        copies[k].wait()
        total = total + choose(send, k * chunk, chunk, held[k * chunk : (k + 1) * chunk, :])
    out_ref[...] = total.astype(BF16)


def hub_start(my_col, owner, rows, table):
    nodes, width = table.shape
    sent = COLS * PAIR
    return pl.pallas_call(
        hub_kernel,
        in_specs=[smem(), vmem(), vmem(), hbm()],
        out_specs=[vmem()] * 4,
        out_shape=[shape(BF16, sent, width), shape(I32, 8, TB), shape(I32, SHARE, 1), shape(I32, HUBS // TB, TB)],
        scratch_shapes=[pltpu.VMEM((nodes, width), BF16), pltpu.SemaphoreType.DMA((SIDE,))],
        compiler_params=params(60),
        cost_estimate=cost(),
        name="hub_start",
    )(my_col, owner, rows, table)


def keep_kernel(keep_ref, arrived_ref, first_ref, second_ref):
    kept = choose(keep_ref[...], 0, arrived_ref.shape[0], arrived_ref[...]).astype(BF16)
    first_ref[...] = kept[:HALF]
    second_ref[...] = kept[HALF:]


def hub_keep(keep_index, arrived):
    half = shape(BF16, HALF, arrived.shape[1])
    return pl.pallas_call(
        keep_kernel,
        in_specs=[vmem(), vmem()],
        out_specs=[vmem(), vmem()],
        out_shape=[half, half],
        compiler_params=params(8),
        cost_estimate=cost(),
        name="hub_keep",
    )(keep_index, arrived)


def halo_kernel(noted, rows_ref, count_ref, table_ref, out_ref, held, wide, picked, staged, sem, out_sem):
    lanes = 4
    unroll = 32
    height = HALO + (NOTE if noted else 0)
    copies = load_table(table_ref, held, sem)
    chunk = held.shape[0] // SIDE
    for k in range(SIDE):
        copies[k].wait()

        @pl.loop(0, chunk // TB)
        def _(n):
            top = pl.multiple_of(k * chunk + n * TB, TB)
            widen(held[pl.ds(top, TB), :].astype(F32), wide, top)

    out = [
        pltpu.make_async_copy(
            staged.at[pl.ds(peer * height, height)], out_ref.at[pl.ds(peer * height, height)], out_sem.at[peer]
        )
        for peer in range(ROWS)
    ]
    for peer in range(ROWS):
        count = count_ref[0, peer]

        @pl.loop(0, (count + unroll - 1) // unroll)
        def _(group):
            for u in range(unroll):
                slot = group * unroll + u
                move_row(wide, rows_ref[peer * HALO + slot], picked, slot)

        for half in range(HALO // TB):
            live = iota((TB, TB), 0) + half * TB < count
            top = peer * height + half * TB
            for j in range(lanes):
                part = picked[pl.ds(half * TB * lanes + j, TB, stride=lanes), :]
                staged[top : top + TB, j * TB : (j + 1) * TB] = jnp.where(live, part, 0.0).astype(BF16)
        if noted:
            top = peer * height + HALO
            staged[top : top + NOTE, :] = jnp.full((NOTE, lanes * TB), count, I32).astype(F32).astype(BF16)
        out[peer].start()
    for copy in out:
        copy.wait()


def halo_start(noted, rows, count, table):
    nodes, width = table.shape
    height = ROWS * (HALO + (NOTE if noted else 0))
    lanes = width // TB
    return pl.pallas_call(
        functools.partial(halo_kernel, noted),
        in_specs=[smem(), smem(), hbm()],
        out_specs=hbm(),
        out_shape=shape(BF16, height, width),
        scratch_shapes=[
            pltpu.VMEM((nodes, width), BF16),
            pltpu.VMEM((nodes * lanes, TB), F32),
            pltpu.VMEM((HALO * lanes, TB), F32),
            pltpu.VMEM((height, width), BF16),
            pltpu.SemaphoreType.DMA((SIDE,)),
            pltpu.SemaphoreType.DMA((ROWS,)),
        ],
        compiler_params=params(60),
        cost_estimate=cost(),
        name="halo_start",
    )(rows, count, table)


def start_chunks(pairs, sem):
    copies = [pltpu.make_async_copy(source, target, sem.at[k]) for k, (source, target) in enumerate(pairs)]
    for copy in copies:
        copy.start()
    return copies


def chunk_copies(source, target, sem):
    return [
        pltpu.make_async_copy(source.at[pl.ds(k * TALL, TALL)], target.at[pl.ds(k * TALL, TALL)], sem.at[k])
        for k in range(source.shape[0] // TALL)
    ]


def gather_blocks(table, cols_ref, block):
    tops = [pl.multiple_of(cols_ref[t, block] * TB, TB) for t in range(2)]
    return jnp.concatenate([table[pl.ds(top, TB), :] for top in tops], axis=0)


def tail_kernel(last, *refs):
    pieces = refs[:8]
    cols_ref, far_ref, pos_ref, halo_ref, table_ref, tiles_ref, far_tiles_ref, weight_ref = refs[8:16]
    rest = refs[16:]
    if last:
        counts, out_ref = rest[:2]
        rest = rest[2:]
    else:
        send_ref, out_ref, picked_ref, counts = rest[:4]
        notes, full = rest[-2:]
        rest = rest[4:-2]
    held, wide, placed, store, table, tiles, far_tiles, weight, joined, result, sem, out_sem = rest
    lanes = 4
    size = HUBS // 8
    width = store.shape[1]
    halo_rows = ROWS * HALO
    height = halo_ref.shape[0] // ROWS
    pairs = [(pieces[k], held.at[pl.ds(k * size, size)]) for k in range(8)]
    pairs += [(table_ref, table), (tiles_ref, tiles), (far_tiles_ref, far_tiles)]
    for p in range(ROWS):
        pairs.append((halo_ref.at[pl.ds(p * height, HALO)], store.at[pl.ds(p * HALO, HALO)]))
        if not last:
            pairs.append((halo_ref.at[pl.ds(p * height + HALO, NOTE)], notes.at[pl.ds(p * NOTE, NOTE)]))
    pairs.append((weight_ref, weight))
    copies = start_chunks(pairs, sem)
    for k in range(8):
        copies[k].wait()
        widen(held[k * size : (k + 1) * size, :].astype(F32), wide, k * size)
    unroll = 64
    for k in range(HUBS // TB):

        @pl.loop(0, TB // unroll)
        def _(n):
            for u in range(unroll):
                slot = n * unroll + u
                move_row(wide, pos_ref[k, slot], placed, k * TB + slot)

    for j in range(lanes):
        store[halo_rows : halo_rows + HUBS, j * TB : (j + 1) * TB] = placed[pl.ds(j, HUBS, stride=lanes), :].astype(BF16)
    for copy in copies[8:]:
        copy.wait()
    if not last:
        for p in range(ROWS):
            counts[p : p + 1, :] = notes[p * NOTE : (p + 1) * NOTE, 0:TB].astype(F32)[0:1, :]
        counts[ROWS : 2 * ROWS, :] = jnp.full((ROWS, TB), 1024.0, F32)
    out = chunk_copies(result, out_ref, out_sem)
    group = TALL // TB
    for k in range(result.shape[0] // TALL):
        for b in range(group):
            block = k * group + b
            near, far = tiles[block], far_tiles[block]
            left = jnp.concatenate([near[0], near[1], far[0], far[1]], axis=1)
            right = jnp.concatenate([gather_blocks(table, cols_ref, block), gather_blocks(store, far_ref, block)], axis=0)
            total_rows = jnp.dot(left, right, preferred_element_type=F32)
            mass = near[0].astype(F32) + near[1].astype(F32)
            for t in range(2):
                col = far_ref[t, block]
                peer = jnp.minimum(lax.shift_right_logical(col, 1), ROWS)
                slots = (iota((1, TB), 1) + lax.bitwise_and(col, 1) * TB).astype(F32)
                mass = mass + jnp.where(slots < counts[pl.ds(peer, 1), :], far[t].astype(F32), 0.0)
            inverse = 1.0 / jnp.sum(mass, axis=1, keepdims=True)
            joined[b * TB : (b + 1) * TB, width : 2 * width] = (total_rows * inverse).astype(BF16)
        span = slice(k * TALL, (k + 1) * TALL)
        joined[:, 0:width] = table[span, :]
        preact = jnp.dot(joined[...], weight[...], preferred_element_type=F32)
        active = jnp.maximum(preact, 0.0)
        scale = lax.rsqrt(jnp.mean(active * active, axis=1, keepdims=True) + 1e-05)
        rows = (active * scale).astype(BF16)
        result[span, :] = rows
        out[k].start()
        if not last:
            widen(rows.astype(F32), full, k * TALL)
    if not last:
        sent = picked_ref.shape[0]
        for k in range(sent // TB):

            @pl.loop(0, TB // unroll)
            def _(n):
                for u in range(unroll):
                    slot = n * unroll + u
                    move_row(full, send_ref[k, slot], placed, k * TB + slot)

        for j in range(lanes):
            picked_ref[:, j * TB : (j + 1) * TB] = placed[pl.ds(j, sent, stride=lanes), :].astype(BF16)
    for copy in out:
        copy.wait()


def tail_part(last, hubs, cols, far_cols, pos, halos, table, tiles, far_tiles, weight, extra):
    nodes, width = table.shape
    lanes = width // TB
    in_specs = [hbm()] * 8 + [smem()] * 3 + [hbm()] * 5 + [vmem() if last else smem()]
    args = [*hubs, cols, far_cols, pos, halos, table, tiles, far_tiles, weight, extra]
    out_specs = [hbm()]
    out_shape = [shape(BF16, nodes, width)]
    scratch = [
        pltpu.VMEM((HUBS, width), BF16),
        pltpu.VMEM((HUBS * lanes, TB), F32),
        pltpu.VMEM((HUBS * lanes, TB), F32),
        pltpu.VMEM((ROWS * HALO + HUBS, width), BF16),
        pltpu.VMEM((nodes, width), BF16),
        pltpu.VMEM(tiles.shape, BF16),
        pltpu.VMEM(far_tiles.shape, BF16),
        pltpu.VMEM(weight.shape, BF16),
        pltpu.VMEM((TALL, 2 * width), BF16),
        pltpu.VMEM((nodes, width), BF16),
        pltpu.SemaphoreType.DMA((32,)),
        pltpu.SemaphoreType.DMA((nodes // TALL,)),
    ]
    if not last:
        sent = COLS * PAIR
        out_specs += [vmem(), vmem()]
        out_shape += [shape(BF16, sent, width), shape(F32, 2 * ROWS, TB)]
        scratch += [pltpu.VMEM((ROWS * NOTE, width), BF16), pltpu.VMEM((nodes * lanes, TB), F32)]
    return pl.pallas_call(
        functools.partial(tail_kernel, last),
        in_specs=in_specs,
        out_specs=out_specs,
        out_shape=out_shape,
        scratch_shapes=scratch,
        compiler_params=params(54),
        cost_estimate=cost(),
        name="tail_part",
    )(*args)


def fetch(array, dz, dy):
    pairs = [
        (((z + dz) % SIDE) * SIDE + (y + dy) % SIDE, z * SIDE + y) for z in range(SIDE) for y in range(SIDE)
    ]
    return lax.ppermute(array, "col", pairs)


def spread_hubs(first, second):
    order = (1, 3, 2)
    near_y = {k: fetch(first, 0, k) for k in order}
    near_z = {k: fetch(second, k, 0) for k in order}
    first_all = jnp.concatenate([first] + [near_y[k] for k in range(1, SIDE)], axis=0)
    second_all = jnp.concatenate([second] + [near_z[k] for k in range(1, SIDE)], axis=0)
    far_z = {k: fetch(first_all, k, 0) for k in order}
    far_y = {k: fetch(second_all, 0, k) for k in order}
    left = [first_all] + [far_z[k] for k in range(1, SIDE)]
    right = [second_all] + [far_y[k] for k in range(1, SIDE)]
    return left + right


def exchange(picked, keep, outgoing):
    width = picked.shape[1]
    arrived = lax.all_to_all(picked.reshape(COLS, PAIR, width), "col", 0, 0, tiled=True)
    arrived, outgoing = lax.optimization_barrier((arrived.reshape(-1, width), outgoing))
    hubs = spread_hubs(*hub_keep(keep, arrived))
    halos = lax.all_to_all(outgoing.reshape(ROWS, -1, width), "row", 0, 0, tiled=True)
    return hubs, halos.reshape(-1, width)


def on_device(
    features,
    w_first,
    w_second,
    send_rows,
    halo_count,
    hub_owner,
    hub_row,
    local_cols,
    local_tiles,
    remote_cols,
    remote_tiles,
):
    my_col = lax.axis_index("col").astype(I32).reshape(1)
    rows = send_rows.reshape(-1)
    cols = local_cols[0].T
    far_cols = remote_cols[0].T
    tiles, far_tiles = local_tiles[0], remote_tiles[0]
    picked, send, keep, pos = hub_start(my_col, hub_owner.reshape(1, -1), hub_row, features)
    hubs, halos = exchange(picked, keep, halo_start(True, rows, halo_count, features))
    middle, picked, counts = tail_part(
        False, hubs, cols, far_cols, pos, halos, features, tiles, far_tiles, w_first, send
    )
    hubs, halos = exchange(picked, keep, halo_start(False, rows, halo_count, middle))
    return tail_part(True, hubs, cols, far_cols, pos, halos, middle, tiles, far_tiles, w_second, counts)[0]


def solution(mesh):
    in_specs = (
        P(("row", "col"), None),
        P(),
        P(),
        P(("row", "col"), None, None),
        P(("row", "col"), None),
        P("row", None, None),
        P("row", None),
        P(("row", "col"), None, None),
        P(("row", "col"), None, None, None, None),
        P(("row", "col"), None, None),
        P(("row", "col"), None, None, None, None),
    )
    out_specs = P(("row", "col"), None)
    return jax.shard_map(on_device, mesh=mesh, in_specs=in_specs, out_specs=out_specs, check_vma=False)
```

```python
import functools

import jax
import jax.numpy as jnp
from jax import lax
from jax.experimental import pallas as pl
from jax.experimental.pallas import tpu as pltpu
from jax.sharding import PartitionSpec as P

F32 = jnp.float32
BF16 = jnp.bfloat16
I32 = jnp.int32
MIB = 1024 * 1024
TB = 128
ROWS = 8
COLS = 16
SIDE = 4
HALO = 256
NOTE = 16
HUBS = 2048
PAIR = 24
SHARE = 128
HALF = 64
TALL = 1024


def params(mib):
    return pltpu.CompilerParams(vmem_limit_bytes=mib * MIB)


def cost():
    return pl.CostEstimate(flops=1000, bytes_accessed=1000, transcendentals=0)


def vmem():
    return pl.BlockSpec(memory_space=pltpu.VMEM)


def smem():
    return pl.BlockSpec(memory_space=pltpu.SMEM)


def hbm():
    return pl.BlockSpec(memory_space=pl.ANY)


def shape(dtype, *dims):
    return jax.ShapeDtypeStruct(dims, dtype)


def iota(dims, dim):
    return lax.broadcasted_iota(I32, dims, dim)


def widen(rows, wide, first):
    lanes = rows.shape[1] // TB
    for j in range(lanes):
        wide[pl.ds(first * lanes + j, rows.shape[0], stride=lanes), :] = rows[:, j * TB : (j + 1) * TB]


def move_row(source, row, target, slot):
    lanes = 4
    target[pl.ds(pl.multiple_of(slot * lanes, lanes), lanes), :] = source[
        pl.ds(pl.multiple_of(row * lanes, lanes), lanes), :
    ]


def write_index(my_col, owner, rows):
    my_z, my_y = my_col // SIDE, lax.rem(my_col, SIDE)
    chunks = HUBS // TB
    owner_id = iota((COLS, TB), 0)
    masks, below = [], jnp.zeros((COLS, TB), F32)
    for c in range(chunks):
        part = owner[:, c * TB : (c + 1) * TB]
        masks.append(jnp.where(part == owner_id, 1.0, 0.0))
        below = below + jnp.where(part < owner_id, 1.0, 0.0)
    offset = jnp.sum(below, axis=1, keepdims=True)
    earlier = jnp.where(iota((TB, TB), 0) < iota((TB, TB), 1), 1.0, 0.0).astype(BF16)
    inside = jnp.dot(jnp.concatenate(masks, axis=0).astype(BF16), earlier, preferred_element_type=F32)
    running = jnp.zeros((COLS, 1), F32)
    ranks, places = [], []
    for c in range(chunks):
        rank = inside[c * COLS : (c + 1) * COLS, :] + running
        ranks.append(jnp.sum(masks[c] * rank, axis=0, keepdims=True))
        places.append(jnp.sum(masks[c] * (rank + offset), axis=0, keepdims=True))
        running = running + jnp.sum(masks[c], axis=1, keepdims=True)
    rank = jnp.concatenate(ranks, axis=0).astype(I32)
    place = jnp.concatenate(places, axis=0).astype(I32)
    who = jnp.concatenate([owner[:, c * TB : (c + 1) * TB] for c in range(chunks)], axis=0)
    local = jnp.concatenate([rows[:, c * TB : (c + 1) * TB] for c in range(chunks)], axis=0).astype(F32)
    holder = lax.bitwise_and(place, COLS - 1)
    share = lax.shift_right_logical(place, 4)
    turn = lax.shift_right_logical(rank, 4)
    slot = jnp.where(who == my_col, holder * PAIR + turn, -1)
    kept = jnp.where(holder == my_col, share, -1)
    arrived = (who * PAIR + turn).astype(F32)

    def pick(keys, values, first):
        wanted = iota((TB, TB), 0) + first
        total = jnp.zeros((TB, TB), F32)
        for c in range(chunks):
            total = total + jnp.where(keys[c : c + 1, :] == wanted, values[c : c + 1, :], 0.0)
        return jnp.sum(total, axis=1, keepdims=True).astype(I32)

    send = jnp.concatenate([pick(slot, local, k * TB) for k in range(COLS * PAIR // TB)], axis=0)
    keep = pick(kept, arrived, 0)
    step_z = lax.bitwise_and(lax.shift_right_logical(holder, 2) - my_z + SIDE, SIDE - 1)
    step_y = lax.bitwise_and(lax.bitwise_and(holder, SIDE - 1) - my_y + SIDE, SIDE - 1)
    first = step_z * 256 + step_y * HALF + share
    second = HUBS // 2 + step_y * 256 + step_z * HALF + share - HALF
    return send, keep, jnp.where(share < HALF, first, second)


def choose(wanted, first, count, rows):
    chosen = jnp.where(wanted - first == iota((wanted.shape[0], count), 1), 1.0, 0.0).astype(BF16)
    return jnp.dot(chosen, rows, preferred_element_type=F32)


def load_table(table_ref, held, sem):
    chunk = held.shape[0] // SIDE
    copies = []
    for k in range(SIDE):
        span = pl.ds(k * chunk, chunk)
        copies.append(pltpu.make_async_copy(table_ref.at[span], held.at[span], sem.at[k]))
    for copy in copies:
        copy.start()
    return copies


def hub_kernel(col_ref, owner_ref, row_ref, table_ref, out_ref, send_ref, keep_ref, pos_ref, held, sem):
    copies = load_table(table_ref, held, sem)
    send, keep, pos = write_index(col_ref[0], owner_ref[...], row_ref[...])
    lists = SIDE - 1
    parts = [send[k * TB : (k + 1) * TB, :].astype(F32) for k in range(lists)]
    square = jnp.concatenate(parts + [jnp.zeros((TB, TB - lists), F32)], axis=1)
    send_ref[...] = square.T[0:8, :].astype(I32)
    keep_ref[...] = keep
    pos_ref[...] = pos
    chunk = held.shape[0] // SIDE
    total = jnp.zeros(out_ref.shape, F32)
    for k in range(SIDE):
        copies[k].wait()
        total = total + choose(send, k * chunk, chunk, held[k * chunk : (k + 1) * chunk, :])
    out_ref[...] = total.astype(BF16)


def hub_start(my_col, owner, rows, table):
    nodes, width = table.shape
    sent = COLS * PAIR
    return pl.pallas_call(
        hub_kernel,
        in_specs=[smem(), vmem(), vmem(), hbm()],
        out_specs=[vmem()] * 4,
        out_shape=[shape(BF16, sent, width), shape(I32, 8, TB), shape(I32, SHARE, 1), shape(I32, HUBS // TB, TB)],
        scratch_shapes=[pltpu.VMEM((nodes, width), BF16), pltpu.SemaphoreType.DMA((SIDE,))],
        compiler_params=params(60),
        cost_estimate=cost(),
        name="hub_start",
    )(my_col, owner, rows, table)


def keep_kernel(keep_ref, arrived_ref, first_ref, second_ref):
    kept = choose(keep_ref[...], 0, arrived_ref.shape[0], arrived_ref[...]).astype(BF16)
    first_ref[...] = kept[:HALF]
    second_ref[...] = kept[HALF:]


def hub_keep(keep_index, arrived):
    half = shape(BF16, HALF, arrived.shape[1])
    return pl.pallas_call(
        keep_kernel,
        in_specs=[vmem(), vmem()],
        out_specs=[vmem(), vmem()],
        out_shape=[half, half],
        compiler_params=params(8),
        cost_estimate=cost(),
        name="hub_keep",
    )(keep_index, arrived)


def halo_kernel(noted, rows_ref, count_ref, table_ref, out_ref, held, wide, picked, staged, sem, out_sem):
    lanes = 4
    unroll = 32
    height = HALO + (NOTE if noted else 0)
    copies = load_table(table_ref, held, sem)
    chunk = held.shape[0] // SIDE
    for k in range(SIDE):
        copies[k].wait()

        @pl.loop(0, chunk // TB)
        def _(n):
            top = pl.multiple_of(k * chunk + n * TB, TB)
            widen(held[pl.ds(top, TB), :].astype(F32), wide, top)

    out = [
        pltpu.make_async_copy(
            staged.at[pl.ds(peer * height, height)], out_ref.at[pl.ds(peer * height, height)], out_sem.at[peer]
        )
        for peer in range(ROWS)
    ]
    for peer in range(ROWS):
        count = count_ref[0, peer]

        @pl.loop(0, (count + unroll - 1) // unroll)
        def _(group):
            for u in range(unroll):
                slot = group * unroll + u
                move_row(wide, rows_ref[peer * HALO + slot], picked, slot)

        for half in range(HALO // TB):
            live = iota((TB, TB), 0) + half * TB < count
            top = peer * height + half * TB
            for j in range(lanes):
                part = picked[pl.ds(half * TB * lanes + j, TB, stride=lanes), :]
                staged[top : top + TB, j * TB : (j + 1) * TB] = jnp.where(live, part, 0.0).astype(BF16)
        if noted:
            top = peer * height + HALO
            staged[top : top + NOTE, :] = jnp.full((NOTE, lanes * TB), count, I32).astype(F32).astype(BF16)
        out[peer].start()
    for copy in out:
        copy.wait()


def halo_start(noted, rows, count, table):
    nodes, width = table.shape
    height = ROWS * (HALO + (NOTE if noted else 0))
    lanes = width // TB
    return pl.pallas_call(
        functools.partial(halo_kernel, noted),
        in_specs=[smem(), smem(), hbm()],
        out_specs=hbm(),
        out_shape=shape(BF16, height, width),
        scratch_shapes=[
            pltpu.VMEM((nodes, width), BF16),
            pltpu.VMEM((nodes * lanes, TB), F32),
            pltpu.VMEM((HALO * lanes, TB), F32),
            pltpu.VMEM((height, width), BF16),
            pltpu.SemaphoreType.DMA((SIDE,)),
            pltpu.SemaphoreType.DMA((ROWS,)),
        ],
        compiler_params=params(60),
        cost_estimate=cost(),
        name="halo_start",
    )(rows, count, table)


def start_chunks(pairs, sem):
    copies = [pltpu.make_async_copy(source, target, sem.at[k]) for k, (source, target) in enumerate(pairs)]
    for copy in copies:
        copy.start()
    return copies


def chunk_copies(source, target, sem):
    return [
        pltpu.make_async_copy(source.at[pl.ds(k * TALL, TALL)], target.at[pl.ds(k * TALL, TALL)], sem.at[k])
        for k in range(source.shape[0] // TALL)
    ]


def gather_blocks(table, cols_ref, block):
    tops = [pl.multiple_of(cols_ref[t, block] * TB, TB) for t in range(2)]
    return jnp.concatenate([table[pl.ds(top, TB), :] for top in tops], axis=0)


def tail_kernel(last, *refs):
    pieces = refs[:8]
    cols_ref, far_ref, pos_ref, halo_ref, table_ref, tiles_ref, far_tiles_ref, weight_ref = refs[8:16]
    rest = refs[16:]
    if last:
        counts, out_ref = rest[:2]
        rest = rest[2:]
    else:
        send_ref, out_ref, picked_ref, counts = rest[:4]
        notes, full = rest[-2:]
        rest = rest[4:-2]
    held, wide, placed, store, table, tiles, far_tiles, weight, joined, result, sem, out_sem = rest
    lanes = 4
    size = HUBS // 8
    width = store.shape[1]
    halo_rows = ROWS * HALO
    height = halo_ref.shape[0] // ROWS
    pairs = [(pieces[k], held.at[pl.ds(k * size, size)]) for k in range(8)]
    pairs += [(table_ref, table), (tiles_ref, tiles), (far_tiles_ref, far_tiles)]
    for p in range(ROWS):
        pairs.append((halo_ref.at[pl.ds(p * height, HALO)], store.at[pl.ds(p * HALO, HALO)]))
        if not last:
            pairs.append((halo_ref.at[pl.ds(p * height + HALO, NOTE)], notes.at[pl.ds(p * NOTE, NOTE)]))
    pairs.append((weight_ref, weight))
    copies = start_chunks(pairs, sem)
    for k in range(8):
        copies[k].wait()
        widen(held[k * size : (k + 1) * size, :].astype(F32), wide, k * size)
    unroll = 64
    for k in range(HUBS // TB):

        @pl.loop(0, TB // unroll)
        def _(n):
            for u in range(unroll):
                slot = n * unroll + u
                move_row(wide, pos_ref[k, slot], placed, k * TB + slot)

    for j in range(lanes):
        store[halo_rows : halo_rows + HUBS, j * TB : (j + 1) * TB] = placed[pl.ds(j, HUBS, stride=lanes), :].astype(BF16)
    for copy in copies[8:]:
        copy.wait()
    if not last:
        for p in range(ROWS):
            counts[p : p + 1, :] = notes[p * NOTE : (p + 1) * NOTE, 0:TB].astype(F32)[0:1, :]
        counts[ROWS : 2 * ROWS, :] = jnp.full((ROWS, TB), 1024.0, F32)
    out = chunk_copies(result, out_ref, out_sem)
    group = TALL // TB
    for k in range(result.shape[0] // TALL):
        for b in range(group):
            block = k * group + b
            near, far = tiles[block], far_tiles[block]
            left = jnp.concatenate([near[0], near[1], far[0], far[1]], axis=1)
            right = jnp.concatenate([gather_blocks(table, cols_ref, block), gather_blocks(store, far_ref, block)], axis=0)
            total_rows = jnp.dot(left, right, preferred_element_type=F32)
            mass = near[0].astype(F32) + near[1].astype(F32)
            for t in range(2):
                col = far_ref[t, block]
                peer = jnp.minimum(lax.shift_right_logical(col, 1), ROWS)
                slots = (iota((1, TB), 1) + lax.bitwise_and(col, 1) * TB).astype(F32)
                mass = mass + jnp.where(slots < counts[pl.ds(peer, 1), :], far[t].astype(F32), 0.0)
            inverse = 1.0 / jnp.sum(mass, axis=1, keepdims=True)
            joined[b * TB : (b + 1) * TB, width : 2 * width] = (total_rows * inverse).astype(BF16)
        span = slice(k * TALL, (k + 1) * TALL)
        joined[:, 0:width] = table[span, :]
        preact = jnp.dot(joined[...], weight[...], preferred_element_type=F32)
        active = jnp.maximum(preact, 0.0)
        scale = lax.rsqrt(jnp.mean(active * active, axis=1, keepdims=True) + 1e-05)
        rows = (active * scale).astype(BF16)
        result[span, :] = rows
        out[k].start()
        if not last:
            widen(rows.astype(F32), full, k * TALL)
    if not last:
        sent = picked_ref.shape[0]
        for k in range(sent // TB):

            @pl.loop(0, TB // unroll)
            def _(n):
                for u in range(unroll):
                    slot = n * unroll + u
                    move_row(full, send_ref[k, slot], placed, k * TB + slot)

        for j in range(lanes):
            picked_ref[:, j * TB : (j + 1) * TB] = placed[pl.ds(j, sent, stride=lanes), :].astype(BF16)
    for copy in out:
        copy.wait()


def tail_part(last, hubs, cols, far_cols, pos, halos, table, tiles, far_tiles, weight, extra):
    nodes, width = table.shape
    lanes = width // TB
    in_specs = [hbm()] * 8 + [smem()] * 3 + [hbm()] * 5 + [vmem() if last else smem()]
    args = [*hubs, cols, far_cols, pos, halos, table, tiles, far_tiles, weight, extra]
    out_specs = [hbm()]
    out_shape = [shape(BF16, nodes, width)]
    scratch = [
        pltpu.VMEM((HUBS, width), BF16),
        pltpu.VMEM((HUBS * lanes, TB), F32),
        pltpu.VMEM((HUBS * lanes, TB), F32),
        pltpu.VMEM((ROWS * HALO + HUBS, width), BF16),
        pltpu.VMEM((nodes, width), BF16),
        pltpu.VMEM(tiles.shape, BF16),
        pltpu.VMEM(far_tiles.shape, BF16),
        pltpu.VMEM(weight.shape, BF16),
        pltpu.VMEM((TALL, 2 * width), BF16),
        pltpu.VMEM((nodes, width), BF16),
        pltpu.SemaphoreType.DMA((32,)),
        pltpu.SemaphoreType.DMA((nodes // TALL,)),
    ]
    if not last:
        sent = COLS * PAIR
        out_specs += [vmem(), vmem()]
        out_shape += [shape(BF16, sent, width), shape(F32, 2 * ROWS, TB)]
        scratch += [pltpu.VMEM((ROWS * NOTE, width), BF16), pltpu.VMEM((nodes * lanes, TB), F32)]
    return pl.pallas_call(
        functools.partial(tail_kernel, last),
        in_specs=in_specs,
        out_specs=out_specs,
        out_shape=out_shape,
        scratch_shapes=scratch,
        compiler_params=params(54),
        cost_estimate=cost(),
        name="tail_part",
    )(*args)


def fetch(array, dz, dy):
    pairs = [
        (((z + dz) % SIDE) * SIDE + (y + dy) % SIDE, z * SIDE + y) for z in range(SIDE) for y in range(SIDE)
    ]
    return lax.ppermute(array, "col", pairs)


def spread_hubs(first, second):
    order = (1, 3, 2)
    near_y = {k: fetch(first, 0, k) for k in order}
    near_z = {k: fetch(second, k, 0) for k in order}
    first_all = jnp.concatenate([first] + [near_y[k] for k in range(1, SIDE)], axis=0)
    second_all = jnp.concatenate([second] + [near_z[k] for k in range(1, SIDE)], axis=0)
    far_z = {k: fetch(first_all, k, 0) for k in order}
    far_y = {k: fetch(second_all, 0, k) for k in order}
    left = [first_all] + [far_z[k] for k in range(1, SIDE)]
    right = [second_all] + [far_y[k] for k in range(1, SIDE)]
    return left + right


def exchange(picked, keep, outgoing):
    width = picked.shape[1]
    arrived = lax.all_to_all(picked.reshape(COLS, PAIR, width), "col", 0, 0, tiled=True)
    first, second = hub_keep(keep, arrived.reshape(-1, width))
    first, second, outgoing = lax.optimization_barrier((first, second, outgoing))
    hubs = spread_hubs(first, second)
    halos = lax.all_to_all(outgoing.reshape(ROWS, -1, width), "row", 0, 0, tiled=True)
    return hubs, halos.reshape(-1, width)


def on_device(
    features,
    w_first,
    w_second,
    send_rows,
    halo_count,
    hub_owner,
    hub_row,
    local_cols,
    local_tiles,
    remote_cols,
    remote_tiles,
):
    my_col = lax.axis_index("col").astype(I32).reshape(1)
    rows = send_rows.reshape(-1)
    cols = local_cols[0].T
    far_cols = remote_cols[0].T
    tiles, far_tiles = local_tiles[0], remote_tiles[0]
    picked, send, keep, pos = hub_start(my_col, hub_owner.reshape(1, -1), hub_row, features)
    hubs, halos = exchange(picked, keep, halo_start(True, rows, halo_count, features))
    middle, picked, counts = tail_part(
        False, hubs, cols, far_cols, pos, halos, features, tiles, far_tiles, w_first, send
    )
    hubs, halos = exchange(picked, keep, halo_start(False, rows, halo_count, middle))
    return tail_part(True, hubs, cols, far_cols, pos, halos, middle, tiles, far_tiles, w_second, counts)[0]


def solution(mesh):
    in_specs = (
        P(("row", "col"), None),
        P(),
        P(),
        P(("row", "col"), None, None),
        P(("row", "col"), None),
        P("row", None, None),
        P("row", None),
        P(("row", "col"), None, None),
        P(("row", "col"), None, None, None, None),
        P(("row", "col"), None, None),
        P(("row", "col"), None, None, None, None),
    )
    out_specs = P(("row", "col"), None)
    return jax.shard_map(on_device, mesh=mesh, in_specs=in_specs, out_specs=out_specs, check_vma=False)
```
